512 devices in a mesh: gy: 64 (over x_lo, z, core), gz: 8 (over x_hi, y).
Axes of the slice: x: 4 (x_hi: 2, x_lo: 2; x = x_hi * 2 + x_lo), y: 4, z: 16, core: 2. Of those that a mesh axis runs over, the one named last changes fastest.
Arguments:
- moments: float32 [10, 16, 64, 4096], P(None, 'gz', 'gy'), may hold values from -0.5 to 1.2, as said below
- wavenumbers: int32 [3, 2048], replicated, may hold values from 0 to 31
- mode_gain: float32 [2048], replicated, may hold values from 0.2 to 2
Outputs:
- final_moments: float32 [10, 16, 64, 4096], P(None, 'gz', 'gy')
- mode_coeffs: float32 [2, 3, 2048], replicated
The draws below stay inside these ranges and needn't reach their ends.
Inputs may be any that keep to these rules, and one draw needn't show every extreme that they name: `moments`: density lies in 0.85 to 1.15 in every cell and each component of j / rho is below 0.2 in magnitude.
All inputs are finite; a program needn't handle non-finite values.
Results may differ from the reference program's by a relative error of at most 0.0003.
Values sent between devices are 32-bit elements; how exact they have to be, the bound alone decides.
No kernel may reach another device: no remote copies, remote signals or barrier semaphores. Data moves between devices by JAX's collectives and lax.ppermute only.
A program may use at most 64 MiB of HBM per device.

```python
import math
import jax
import jax.numpy as jnp
from jax import lax

NX = 4096
CZ = 2
K = 2048
KMAX = 32
STEPS = 3
NY = 64
NZ = 16
N_GY = 64
N_GZ = 8


PAIR_LIST = ((0, 0), (1, 1), (2, 2), (0, 1), (0, 2), (1, 2))


MODE_AMPLITUDE = 0.02


def common_waves(key):
    waves = jax.random.randint(jax.random.fold_in(key, 5), (3, K), 0, KMAX, dtype=jnp.int32)
    waves = waves.at[0, 0].set(0)
    waves = waves.at[0, 1].set(KMAX - 1)
    return waves


def draw_wavenumbers(key, part):
    return common_waves(key)


def draw_moments(key, part):
    waves = common_waves(key)
    subkeys = jax.random.split(jax.random.fold_in(key, 11), 3)
    grid_shape = (NZ, NY, NX)
    density = jax.random.uniform(subkeys[0], grid_shape, jnp.float32, 0.85, 1.15)
    noise = jnp.clip(0.015 * jax.random.normal(subkeys[1], (3,) + grid_shape, jnp.float32), -0.04, 0.04)
    x_pos = jnp.arange(NX, dtype=jnp.int32)[None, None, :]
    y_pos = jnp.arange(NY, dtype=jnp.int32)[None, :, None]
    z_pos = jnp.arange(NZ, dtype=jnp.int32)[:, None, None]
    envelope = 1.0 + 0.9 * jnp.cos(2.0 * math.pi * y_pos.astype(jnp.float32) / NY)
    coherent = jnp.zeros(grid_shape, jnp.float32)
    for index_m in range(4):
        fraction = (x_pos * waves[0, index_m] % NX).astype(jnp.float32) / NX
        fraction = fraction + (y_pos * waves[1, index_m] % NY).astype(jnp.float32) / NY
        fraction = fraction + (z_pos * waves[2, index_m] % NZ).astype(jnp.float32) / NZ
        coherent = coherent + jnp.cos(2.0 * math.pi * fraction)
    coherent = MODE_AMPLITUDE * envelope * coherent
    velocity_field = noise + coherent[None]
    nonequil = jnp.clip(0.01 * jax.random.normal(subkeys[2], (6,) + grid_shape, jnp.float32), -0.04, 0.04)
    components = [density] + [density * velocity_field[comp_a] for comp_a in range(3)]
    for index_p, (comp_a, comp_b) in enumerate(PAIR_LIST):
        second = density * velocity_field[comp_a] * velocity_field[comp_b] + nonequil[index_p]
        if comp_a == comp_b:
            second = second + density / 3.0
        components.append(second)
    return jnp.stack(components).astype(jnp.float32)


def setup_inputs(seed: int = 0) -> dict:
    seeds = jax.random.split(jax.random.key(seed), 4)
    moments = draw_moments(jax.random.fold_in(seeds[3], 71), 0)
    wavenumbers = draw_wavenumbers(jax.random.fold_in(seeds[3], 71), 0)
    mode_gain = jnp.clip(jnp.exp(jax.random.uniform(seeds[2], (K,), jnp.float32, math.log(0.2), math.log(2.0))), 0.2, 2.0)
    return {"moments": moments, "wavenumbers": wavenumbers, "mode_gain": mode_gain}


VELOCITIES = ((0, 0, 0), (1, 0, 0), (-1, 0, 0), (0, 1, 0), (0, -1, 0), (0, 0, 1), (0, 0, -1), (1, 1, 0), (-1, -1, 0), (1, -1, 0), (-1, 1, 0), (1, 0, 1), (-1, 0, -1), (1, 0, -1), (-1, 0, 1), (0, 1, 1), (0, -1, -1), (0, 1, -1), (0, -1, 1))
PAIR_LIST = ((0, 0), (1, 1), (2, 2), (0, 1), (0, 2), (1, 2))
RELAX_RATE = 1.6
FORCE_GAIN = 0.5
HIGHEST = lax.Precision.HIGHEST

def lattice_weight(velocity):
    total = abs(velocity[0]) + abs(velocity[1]) + abs(velocity[2])
    if total == 0:
        return 1.0 / 3.0
    if total == 1:
        return 1.0 / 18.0
    return 1.0 / 36.0

def populate(moment_list, velocity):
    density = moment_list[0]
    linear = density
    for comp_a in range(3):
        if velocity[comp_a] != 0:
            linear = linear + 3.0 * velocity[comp_a] * moment_list[1 + comp_a]
    quadratic = jnp.zeros_like(density)
    for index_p, (comp_a, comp_b) in enumerate(PAIR_LIST):
        if comp_a == comp_b:
            factor = velocity[comp_a] * velocity[comp_a] - 1.0 / 3.0
            quadratic = quadratic + factor * (moment_list[4 + index_p] - density / 3.0)
        else:
            factor = 2.0 * velocity[comp_a] * velocity[comp_b]
            if factor != 0:
                quadratic = quadratic + factor * moment_list[4 + index_p]
    return lattice_weight(velocity) * (linear + 4.5 * quadratic)

def add_population(totals, population, velocity):
    totals[0] = totals[0] + population
    for comp_a in range(3):
        if velocity[comp_a] != 0:
            totals[1 + comp_a] = totals[1 + comp_a] + velocity[comp_a] * population
    for index_p, (comp_a, comp_b) in enumerate(PAIR_LIST):
        product = velocity[comp_a] * velocity[comp_b]
        if product != 0:
            totals[4 + index_p] = totals[4 + index_p] + product * population
    return totals

def collide(totals, force_field):
    density = totals[0]
    shifted = [(totals[1 + comp_a] + 0.5 * force_field[comp_a]) / density for comp_a in range(3)]
    result_list = [density] + [totals[1 + comp_a] + force_field[comp_a] for comp_a in range(3)]
    for index_p, (comp_a, comp_b) in enumerate(PAIR_LIST):
        equilibrium = density * shifted[comp_a] * shifted[comp_b]
        if comp_a == comp_b:
            equilibrium = equilibrium + density / 3.0
        result_list.append(equilibrium + (1.0 - RELAX_RATE) * (totals[4 + index_p] - equilibrium))
    return jnp.stack(result_list)

def phase_x(positions, length):
    wave_list = jnp.arange(KMAX, dtype=jnp.int32)
    fraction = (positions[:, None] * wave_list[None, :] % length).astype(jnp.float32) / length
    phase_angle = 2.0 * math.pi * fraction
    return jnp.concatenate([jnp.cos(phase_angle), jnp.sin(phase_angle)], axis=1)

def select_table(wavenumbers):
    wave_list = jnp.arange(KMAX, dtype=jnp.int32)
    return (wave_list[:, None] == wavenumbers[0][None, :]).astype(jnp.float32)

def phase_yz(wavenumbers, y_positions, y_length, z_positions, z_length):
    fraction = (y_positions[None, :, None] * wavenumbers[1][None, None, :] % y_length).astype(jnp.float32) / y_length
    fraction = fraction + (z_positions[:, None, None] * wavenumbers[2][None, None, :] % z_length).astype(jnp.float32) / z_length
    phase_angle = 2.0 * math.pi * fraction
    return (jnp.cos(phase_angle), jnp.sin(phase_angle))

def project(velocity_field, x_basis, selector, cos_yz, sin_yz):
    modes = cos_yz.shape[-1]
    depth, rows, cells_x = velocity_field.shape[1:]
    waves = x_basis.shape[1] // 2
    projected = jnp.dot(velocity_field.reshape(-1, cells_x), x_basis, precision=HIGHEST, preferred_element_type=jnp.float32)
    cos_x = jnp.dot(projected[:, :waves], selector, precision=HIGHEST, preferred_element_type=jnp.float32).reshape(3, depth, rows, modes)
    sin_x = jnp.dot(projected[:, waves:], selector, precision=HIGHEST, preferred_element_type=jnp.float32).reshape(3, depth, rows, modes)
    cos_sum = lax.optimization_barrier(jnp.sum(cos_x * cos_yz - sin_x * sin_yz, axis=(1, 2)))
    sin_sum = lax.optimization_barrier(jnp.sum(sin_x * cos_yz + cos_x * sin_yz, axis=(1, 2)))
    return jnp.stack([cos_sum, sin_sum])

def apply_force(scaled, x_basis, selector, cos_yz, sin_yz):
    depth, rows, modes = cos_yz.shape
    cos_part = scaled[0][:, None, None, :]
    sin_part = scaled[1][:, None, None, :]
    part_a = (cos_part * cos_yz + sin_part * sin_yz).reshape(-1, modes)
    part_b = (sin_part * cos_yz - cos_part * sin_yz).reshape(-1, modes)
    wave_a = jnp.dot(part_a, selector.T, precision=HIGHEST, preferred_element_type=jnp.float32)
    wave_b = jnp.dot(part_b, selector.T, precision=HIGHEST, preferred_element_type=jnp.float32)
    stacked = jnp.concatenate([wave_a, wave_b], axis=-1)
    return jnp.dot(stacked, x_basis.T, precision=HIGHEST, preferred_element_type=jnp.float32).reshape(3, depth, rows, x_basis.shape[0])

def reference(moments, wavenumbers, mode_gain):
    cells_z, cells_y, cells_x = moments.shape[1:]
    x_basis = phase_x(jnp.arange(cells_x, dtype=jnp.int32), cells_x)
    selector = select_table(wavenumbers)
    y_positions = jnp.arange(cells_y, dtype=jnp.int32)
    normalizer = 1.0 / math.sqrt(NX * NY * NZ)
    force_scale = FORCE_GAIN / math.sqrt(2 * K * N_GY * N_GZ)
    blocks = jnp.arange(cells_z // CZ, dtype=jnp.int32)
    moment_state = moments
    coeffs = jnp.zeros((2, 3, K), jnp.float32)
    for step_index in range(STEPS):
        velocity_field = moment_state[1:4] / moment_state[0]

        def block_tables(block_index):
            z_start = (block_index * CZ).astype(jnp.int32)
            z_positions = z_start + jnp.arange(CZ, dtype=jnp.int32)
            return (z_start, phase_yz(wavenumbers, y_positions, cells_y, z_positions, cells_z))

        def block_sum(block_index):
            z_start, tables = block_tables(block_index)
            piece = lax.dynamic_slice_in_dim(velocity_field, z_start, CZ, 1)
            return project(piece, x_basis, selector, tables[0], tables[1])
        coeffs = lax.optimization_barrier(jnp.sum(lax.map(block_sum, blocks), axis=0)) * normalizer
        scaled = coeffs * mode_gain[None, None, :] * force_scale

        def block_force(block_index):
            z_start, tables = block_tables(block_index)
            return apply_force(scaled, x_basis, selector, tables[0], tables[1])
        force_blocks = lax.map(block_force, blocks)
        force_field = jnp.transpose(force_blocks, (1, 0, 2, 3, 4)).reshape(3, cells_z, cells_y, cells_x)
        totals = [jnp.zeros((cells_z, cells_y, cells_x), jnp.float32) for index_p in range(10)]
        for velocity in VELOCITIES:
            population = populate(moment_state, velocity)
            read = jnp.roll(population, (velocity[2], velocity[1], velocity[0]), axis=(0, 1, 2))
            totals = add_population(totals, read, velocity)
        moment_state = collide(totals, force_field)
    return (moment_state, coeffs)
```

```python
import itertools
import math

import jax
import jax.numpy as jnp
import ml_dtypes
import numpy as np
from jax import lax
from jax.experimental import pallas as pl
from jax.experimental.pallas import tpu as pltpu
from jax.sharding import PartitionSpec as P

KMAX = 32
STEPS = 3
RELAX_RATE = 1.6
FORCE_GAIN = 0.5
LANES = 128
F32 = jnp.float32
BF16 = jnp.bfloat16

PART_SIZES = {"xl": 2, "z": 16, "c": 2, "xh": 2, "y": 4}
DEPTH = 16
FAN = 32

PAIR_LIST = ((0, 0), (1, 1), (2, 2), (0, 1), (0, 2), (1, 2))
PAIR_INDEX = {(0, 1): 7, (0, 2): 8, (1, 2): 9}


def device_groups(axes):
    others = [a for a in PART_SIZES if a not in axes]
    groups = []
    for outer in itertools.product(*[range(PART_SIZES[a]) for a in others]):
        group = []
        for inner in itertools.product(*[range(PART_SIZES[a]) for a in axes]):
            at = dict(zip(others, outer))
            at.update(zip(axes, inner))
            gy = at["xl"] * 32 + at["z"] * 2 + at["c"]
            gz = at["xh"] * 4 + at["y"]
            group.append(gy * 8 + gz)
        groups.append(group)
    return groups


def split_np(values):
    high = values.astype(ml_dtypes.bfloat16)
    low = (values - high.astype(np.float64)).astype(ml_dtypes.bfloat16)
    return high, low


def split(value):
    high = value.astype(BF16)
    low = (value - high.astype(F32)).astype(BF16)
    return high, low


def static_tables(cells_x, cells_y, cells_z):
    wave = np.arange(KMAX)
    lane = np.arange(LANES)
    rows = cells_x // LANES
    angle = 2.0 * np.pi * (lane[:, None] * wave[None, :] % cells_x) / cells_x
    basis = np.concatenate([np.cos(angle), np.sin(angle)], axis=1)
    high, low = split_np(basis)
    forward = np.concatenate([high, high, low, low], axis=1)
    backward = np.concatenate(
        [np.concatenate([high.T, high.T], axis=0), np.concatenate([low.T, low.T], axis=0)], axis=1
    )
    row = np.arange(rows)
    turn = 2.0 * np.pi * (row[:, None] * LANES * wave[None, :] % cells_x) / cells_x
    turn_c = np.tile(np.cos(turn), (1, 4)).astype(np.float32)
    turn_s = np.concatenate([-np.sin(turn), np.sin(turn)] * 2, axis=1).astype(np.float32)
    d_y = np.arange(cells_y)[:, None, None]
    d_z = (2 * np.arange(cells_z // 2)[None, :] + np.arange(2)[:, None])[None]
    d_y, d_z = np.broadcast_arrays(d_y, d_z)
    k_y = np.repeat(np.arange(KMAX), cells_z)
    k_z = np.tile(np.arange(cells_z), KMAX)
    beta = 2.0 * np.pi * (
        (d_y.reshape(-1, 1) * k_y % cells_y) / cells_y + (d_z.reshape(-1, 1) * k_z % cells_z) / cells_z
    )
    grid_c = np.concatenate(split_np(np.cos(beta)), axis=0)
    grid_s = np.concatenate(split_np(np.sin(beta)), axis=0)
    return forward, backward, turn_c, turn_s, grid_c, grid_s


def lane_index(shape):
    return lax.broadcasted_iota(jnp.int32, shape, len(shape) - 1)


def call(kernel, out_shapes, name, flops=0, moved=0, scratch=()):
    single = not isinstance(out_shapes, (list, tuple))
    shapes = [out_shapes] if single else list(out_shapes)
    spec = pl.BlockSpec(memory_space=pltpu.VMEM)
    return pl.pallas_call(
        kernel,
        out_shape=out_shapes if single else tuple(shapes),
        out_specs=spec if single else tuple(spec for _ in shapes),
        scratch_shapes=list(scratch),
        compiler_params=pltpu.CompilerParams(vmem_limit_bytes=40 * 1024 * 1024),
        name=name,
    )


def sds(shape, dtype=F32):
    return jax.ShapeDtypeStruct(shape, dtype)


def setup_kernel(scale, sizes, waves_ref, gain_ref, grid_c_ref, grid_s_ref, ta_ref, tb_ref, pc_ref, ps_ref):
    cells_y, cells_z = sizes
    modes = gain_ref.shape[1]
    k_x = waves_ref[0:1, :]
    k_y = waves_ref[1:2, :]
    k_z = waves_ref[2:3, :]
    cell = k_y * cells_z + lax.rem(k_z, cells_z)
    columns = KMAX * cells_z
    hot_yz = (lax.broadcasted_iota(jnp.int32, (columns, modes), 0) == cell).astype(F32).astype(BF16)
    wave_row = lax.rem(lax.broadcasted_iota(jnp.int32, (LANES, modes), 0), KMAX)
    gains = jnp.where(wave_row == k_x, gain_ref[0:1, :], 0.0)
    gain_high, gain_low = split(gains)
    dims = (((1,), (1,)), ((), ()))
    spectrum = lax.dot_general(hot_yz, gain_high, dims, preferred_element_type=F32)
    spectrum = spectrum + lax.dot_general(hot_yz, gain_low, dims, preferred_element_type=F32)
    spec_high, spec_low = split(spectrum * scale)
    count = grid_c_ref.shape[0] // 2
    for grid_ref, out_ref in ((grid_c_ref, ta_ref), (grid_s_ref, tb_ref)):
        high = grid_ref[0:count, :]
        table = jnp.dot(high, spec_high, preferred_element_type=F32)
        table = table + jnp.dot(high, spec_low, preferred_element_type=F32)
        table = table + jnp.dot(grid_ref[count:, :], spec_high, preferred_element_type=F32)
        out_ref[...] = table.reshape(out_ref.shape)
    lanes = lane_index((8, LANES))
    lower = lanes < LANES // 2
    sign = jnp.where(lax.rem(lanes, 2 * KMAX) < KMAX, 1.0, -1.0)

    def fix(index, carry):
        for ref, factor in ((ta_ref, None), (tb_ref, sign)):
            even = ref[index, 0]
            odd = ref[index, 1]
            new_even = jnp.where(lower, even, pltpu.roll(odd, 1, 0))
            new_odd = jnp.where(lower, odd, even)
            if factor is not None:
                new_even = new_even * factor
                new_odd = new_odd * factor
            ref[index, 0] = new_even
            ref[index, 1] = new_odd
        return carry

    lax.fori_loop(0, cells_y, fix, 0)
    gy = lax.axis_index("gy")
    gz = lax.axis_index("gz")
    row = lax.broadcasted_iota(jnp.int32, (2 * DEPTH, modes), 0)
    y_pos = (gy // 32) * 32 + lax.rem(gy, 2) + 2 * lax.rem(row, DEPTH)
    z_pos = 2 * gz + row // DEPTH
    turns = lax.rem(y_pos * k_y, cells_y).astype(F32) / cells_y
    turns = turns + lax.rem(z_pos * k_z, cells_z).astype(F32) / cells_z
    phase = 2.0 * math.pi * turns
    pc_ref[...] = jnp.cos(phase)
    ps_ref[...] = jnp.sin(phase)


def project(velocity, forward_ref, turn_c_ref, turn_s_ref):
    stacked = jnp.concatenate(velocity, axis=0)
    high, low = split(stacked)
    both = jnp.concatenate([high, low], axis=0)
    product = jnp.dot(both, forward_ref[...], preferred_element_type=F32)
    count = stacked.shape[0]
    base = product[:count, :LANES] + product[count:, :LANES]
    base = base + (product[:count, LANES:] + product[count:, LANES:])
    swapped = pltpu.roll(base, KMAX, 1)
    rows = turn_c_ref.shape[0]
    turn_c = turn_c_ref[...]
    turn_s = turn_s_ref[...]
    lower = lane_index((1, LANES)) < LANES // 2
    parts = []
    for comp in range(3):
        sums = []
        for layer in range(2):
            start = (2 * comp + layer) * rows
            term = base[start : start + rows] * turn_c + swapped[start : start + rows] * turn_s
            sums.append(jnp.sum(term, axis=0, keepdims=True))
        parts.append(jnp.where(lower, sums[0], sums[1]))
    return jnp.concatenate(parts, axis=1)


def first_kernel(state_ref, forward_ref, turn_c_ref, turn_s_ref, send_ref):
    inverse = 1.0 / state_ref[0]
    velocity = [state_ref[1 + comp] * inverse for comp in range(3)]
    row = project(velocity, forward_ref, turn_c_ref, turn_s_ref)
    send_ref[...] = jnp.broadcast_to(row, send_ref.shape)


def convolve(recv_ref, ta_ref, tb_ref, cells_y):
    gy = lax.axis_index("gy")
    own_xl = gy // 32
    own_z = lax.rem(gy, 32) // 2
    own_c = lax.rem(gy, 2)
    lanes = lane_index((DEPTH, LANES))
    first = lax.rem(lanes, 2 * KMAX) < KMAX
    direct = []
    swapped = []
    for comp in range(3):
        block = recv_ref[:, comp * LANES : (comp + 1) * LANES]
        direct.append(block)
        swapped.append(jnp.where(first, pltpu.roll(block, LANES - KMAX, 1), pltpu.roll(block, KMAX, 1)))
    acc = {}
    for source in range(DEPTH):
        d_row = [jnp.broadcast_to(direct[comp][source : source + 1, :], (8, LANES)) for comp in range(3)]
        s_row = [jnp.broadcast_to(swapped[comp][source : source + 1, :], (8, LANES)) for comp in range(3)]
        for j, (xl, c) in enumerate(itertools.product(range(2), range(2))):
            shift = 32 * (xl - own_xl) + 2 * (own_z - source) + (c - own_c)
            shift = lax.rem(shift + 2 * cells_y, cells_y)
            for par in range(2):
                t_a = ta_ref[shift, par]
                t_b = tb_ref[shift, par]
                for comp in range(3):
                    term = t_a * d_row[comp] + t_b * s_row[comp]
                    key = (j, par, comp)
                    acc[key] = term if source == 0 else acc[key] + term
    return acc


def write_partial(acc, send_ref):
    gz = lax.axis_index("gz")
    lower = lane_index((8, LANES)) < LANES // 2
    for j in range(4):
        for comp in range(3):
            even = acc[(j, 0, comp)]
            odd = acc[(j, 1, comp)]
            even = even + pltpu.roll(even, LANES // 2, 1)
            odd = odd + pltpu.roll(odd, LANES // 2, 1)
            block = pltpu.roll(jnp.where(lower, even, odd), gz, 0)
            send_ref[j * 8 : (j + 1) * 8, comp * LANES : (comp + 1) * LANES] = block


def middle_kernel(cells_y, recv_ref, ta_ref, tb_ref, send_ref):
    write_partial(convolve(recv_ref, ta_ref, tb_ref, cells_y), send_ref)


def last_middle_kernel(cells_y, norm, recv_ref, ta_ref, tb_ref, waves_ref, pc_ref, ps_ref, send_ref):
    write_partial(convolve(recv_ref, ta_ref, tb_ref, cells_y), send_ref)
    modes = waves_ref.shape[1]
    lanes = lane_index((DEPTH, LANES)) // KMAX
    blocks = []
    for comp in range(3):
        block = recv_ref[:, comp * LANES : (comp + 1) * LANES]
        for part in range(4):
            blocks.append(jnp.where(lanes == part, block, 0.0))
    stacked = jnp.concatenate(blocks, axis=0)
    high, low = split(stacked)
    both = jnp.concatenate([high, low], axis=0)
    wave_row = lax.rem(lax.broadcasted_iota(jnp.int32, (LANES, modes), 0), KMAX)
    hot = (wave_row == waves_ref[0:1, :]).astype(F32).astype(BF16)
    picked = jnp.dot(both, hot, preferred_element_type=F32)
    count = stacked.shape[0]
    picked = picked[:count] + picked[count:]
    for comp in range(3):
        cos_sum = None
        sin_sum = None
        for layer in range(2):
            start = (comp * 4 + layer * 2) * DEPTH
            cos_x = picked[start : start + DEPTH]
            sin_x = picked[start + DEPTH : start + 2 * DEPTH]
            cos_yz = pc_ref[layer * DEPTH : (layer + 1) * DEPTH, :]
            sin_yz = ps_ref[layer * DEPTH : (layer + 1) * DEPTH, :]
            cos_term = cos_x * cos_yz - sin_x * sin_yz
            sin_term = sin_x * cos_yz + cos_x * sin_yz
            cos_sum = cos_term if cos_sum is None else cos_sum + cos_term
            sin_sum = sin_term if sin_sum is None else sin_sum + sin_term
        for part, total in ((0, cos_sum), (1, sin_sum)):
            total = jnp.sum(total, axis=0, keepdims=True) * norm
            for tile in range(modes // LANES):
                index = (part * 3 + comp) * (modes // LANES) + tile
                dest, slot = divmod(index, 3)
                send_ref[dest : dest + 1, (3 + slot) * LANES : (4 + slot) * LANES] = total[
                    :, tile * LANES : (tile + 1) * LANES
                ]


def weight(velocity):
    total = sum(abs(v) for v in velocity)
    return (1.0 / 3.0, 1.0 / 18.0, 1.0 / 36.0)[total]


class Populations:
    def __init__(self, fields):
        self.fields = fields
        third = fields[0] * (1.0 / 3.0)
        self.normal = [fields[4 + comp] - third for comp in range(3)]
        self.trace = (self.normal[0] + self.normal[1] + self.normal[2]) * (1.0 / 3.0)
        self.halves = {}

    def half(self, velocity):
        if velocity not in self.halves:
            quad = -self.trace
            flow = None
            used = [comp for comp in range(3) if velocity[comp] != 0]
            for comp in used:
                quad = quad + self.normal[comp]
                term = self.fields[1 + comp] if velocity[comp] > 0 else -self.fields[1 + comp]
                flow = term if flow is None else flow + term
            if len(used) == 2:
                factor = 2.0 * velocity[used[0]] * velocity[used[1]]
                quad = quad + factor * self.fields[PAIR_INDEX[tuple(used)]]
            w = weight(velocity)
            even = w * self.fields[0] + (4.5 * w) * quad
            odd = None if flow is None else (3.0 * w) * flow
            self.halves[velocity] = (even, odd)
        return self.halves[velocity]

    def get(self, velocity):
        flip = next((v < 0 for v in velocity if v != 0), False)
        key = tuple(-v for v in velocity) if flip else velocity
        even, odd = self.half(key)
        value = even if odd is None else (even - odd if flip else even + odd)
        if velocity[0] == 0:
            return value
        rows = value.shape[0]
        lanes = lane_index(value.shape)
        if velocity[0] > 0:
            moved = pltpu.roll(value, 1, 1)
            return jnp.where(lanes == 0, pltpu.roll(moved, 1, 0), moved)
        moved = pltpu.roll(value, LANES - 1, 1)
        return jnp.where(lanes == LANES - 1, pltpu.roll(moved, rows - 1, 0), moved)


def layers(state_ref):
    rows = state_ref.shape[1] // 2
    return [
        Populations([state_ref[field, layer * rows : (layer + 1) * rows, :] for field in range(10)])
        for layer in range(2)
    ]


def face_z(sign):
    return ((0, 0, sign), (1, 0, sign), (-1, 0, sign), (0, 1, sign), (0, -1, sign))


def face_y(sign):
    return ((0, sign, 0), (1, sign, 0), (-1, sign, 0))


def faces_kernel(state_ref, zup_ref, zdn_ref, yup_ref, ydn_ref):
    low, high = layers(state_ref)
    for index, velocity in enumerate(face_z(1)):
        zup_ref[index] = high.get(velocity)
    for index, velocity in enumerate(face_z(-1)):
        zdn_ref[index] = low.get(velocity)
    for sign, ref in ((1, yup_ref), (-1, ydn_ref)):
        for index, velocity in enumerate(face_y(sign)):
            ref[2 * index] = low.get(velocity)
            ref[2 * index + 1] = high.get(velocity)
        ref[6] = low.get((0, sign, 1))
        ref[7] = high.get((0, sign, -1))


def stream_kernel(state_ref, zup_ref, zdn_ref, yup_ref, ydn_ref, total_ref):
    own = layers(state_ref)
    rows = state_ref.shape[1] // 2
    for layer in range(2):
        terms = {}
        for velocity in ((0, 0, 0), (1, 0, 0), (-1, 0, 0)):
            terms[velocity] = own[layer].get(velocity)
        for index in range(3):
            up = face_z(1)[index]
            down = face_z(-1)[index]
            terms[up] = zup_ref[index] if layer == 0 else own[0].get(up)
            terms[down] = own[1].get(down) if layer == 0 else zdn_ref[index]
        for sign, ref in ((1, yup_ref), (-1, ydn_ref)):
            for index, velocity in enumerate(face_y(sign)):
                terms[velocity] = ref[2 * index + layer]
            terms[(0, sign, 1)] = ref[8] if layer == 0 else ref[6]
            terms[(0, sign, -1)] = ref[7] if layer == 0 else ref[9]
        total = [None] * 10

        def add(index, value, factor=1):
            if factor < 0:
                total[index] = -value if total[index] is None else total[index] - value
            else:
                total[index] = value if total[index] is None else total[index] + value

        for velocity, value in terms.items():
            add(0, value)
            for comp in range(3):
                if velocity[comp] != 0:
                    add(1 + comp, value, velocity[comp])
            for index, (comp_a, comp_b) in enumerate(PAIR_LIST):
                product = velocity[comp_a] * velocity[comp_b]
                if product != 0:
                    add(4 + index, value, product)
        for index in range(10):
            total_ref[index, layer * rows : (layer + 1) * rows, :] = total[index]


def expand(row, backward_ref, turn_c_ref, turn_s_ref):
    turn_c = turn_c_ref[...]
    turn_s = turn_s_ref[...]
    lower = lane_index((1, LANES)) < LANES // 2
    blocks = []
    for comp in range(3):
        pair = row[:, comp * LANES : (comp + 1) * LANES]
        other = pltpu.roll(pair, LANES // 2, 1)
        for value in (jnp.where(lower, pair, other), jnp.where(lower, other, pair)):
            blocks.append(value * turn_c - pltpu.roll(value, KMAX, 1) * turn_s)
    stacked = jnp.concatenate(blocks, axis=0)
    high = stacked.astype(BF16).astype(F32)
    mixed = jnp.where(lane_index(stacked.shape) < LANES // 2, high, stacked - high).astype(BF16)
    product = jnp.dot(mixed, backward_ref[...], preferred_element_type=F32)
    return product[:, :LANES] + product[:, LANES:]


def collide_kernel(
    last, recv_ref, total_ref, backward_ref, forward_ref, turn_c_ref, turn_s_ref, state_ref, send_ref
):
    row = jnp.sum(recv_ref[...], axis=0, keepdims=True)
    force = expand(row[:, : 3 * LANES], backward_ref, turn_c_ref, turn_s_ref)
    cells = total_ref.shape[1]
    density = total_ref[0]
    inverse = 1.0 / density
    state_ref[0] = density
    shifted = []
    velocity = []
    for comp in range(3):
        part = force[comp * cells : (comp + 1) * cells]
        flow = total_ref[1 + comp]
        shifted.append((flow + 0.5 * part) * inverse)
        flow = flow + part
        state_ref[1 + comp] = flow
        velocity.append(flow * inverse)
    for index, (comp_a, comp_b) in enumerate(PAIR_LIST):
        equilibrium = density * shifted[comp_a] * shifted[comp_b]
        if comp_a == comp_b:
            equilibrium = equilibrium + density * (1.0 / 3.0)
        state_ref[4 + index] = equilibrium + (1.0 - RELAX_RATE) * (total_ref[4 + index] - equilibrium)
    if last:
        send_ref[...] = jnp.broadcast_to(row[:, 3 * LANES :], send_ref.shape)
    else:
        row = project(velocity, forward_ref, turn_c_ref, turn_s_ref)
        send_ref[...] = jnp.broadcast_to(row, send_ref.shape)


def coeffs_kernel(recv_ref, out_ref):
    tiles = out_ref.shape[2] // LANES
    for part in range(2):
        for comp in range(3):
            for tile in range(tiles):
                dest, slot = divmod((part * 3 + comp) * tiles + tile, 3)
                out_ref[part, comp : comp + 1, tile * LANES : (tile + 1) * LANES] = recv_ref[
                    dest : dest + 1, slot * LANES : (slot + 1) * LANES
                ]


def ring(count, step):
    return [(index, (index + step) % count) for index in range(count)]


def per_device(moments, wavenumbers, mode_gain):
    depth, rows, cells_x = moments.shape[1:]
    modes = mode_gain.shape[0]
    count_gy = lax.axis_size("gy")
    count_gz = lax.axis_size("gz")
    cells_y = rows * count_gy
    cells_z = depth * count_gz
    x_rows = cells_x // LANES
    norm = 1.0 / math.sqrt(cells_x * cells_y * cells_z)
    force_scale = FORCE_GAIN / math.sqrt(2 * modes * count_gy * count_gz)
    tables = [jnp.asarray(t) for t in static_tables(cells_x, cells_y, cells_z)]
    forward, backward, turn_c, turn_s, grid_c, grid_s = tables
    state = moments.reshape(10, depth * x_rows, LANES)
    deep = device_groups(["z"])
    wide = device_groups(["xl", "c", "xh", "y"])

    def exchange(value, groups):
        return lax.all_to_all(value, ("gy", "gz"), 0, 0, tiled=True, axis_index_groups=groups)

    layer = (x_rows, LANES)
    send = call(first_kernel, sds((DEPTH, 3 * LANES)), "first")(state, forward, turn_c, turn_s)
    ta, tb, pc, ps = call(
        lambda *refs: setup_kernel(norm * force_scale, (cells_y, cells_z), *refs),
        [sds((cells_y, 2, 8, LANES))] * 2 + [sds((2 * DEPTH, modes))] * 2,
        "setup",
    )(wavenumbers, mode_gain.reshape(1, modes), grid_c, grid_s)
    for step in range(STEPS):
        last = step == STEPS - 1
        recv = exchange(send, deep)
        zup, zdn, yup, ydn = call(
            faces_kernel, [sds((5,) + layer)] * 2 + [sds((8,) + layer)] * 2, "faces"
        )(state)
        zup = lax.ppermute(zup, "gz", ring(count_gz, 1))
        zdn = lax.ppermute(zdn, "gz", ring(count_gz, -1))
        yup = jnp.concatenate([yup, zup[3:4], zdn[3:4]], axis=0)
        ydn = jnp.concatenate([ydn, zup[4:5], zdn[4:5]], axis=0)
        yup = lax.ppermute(yup, "gy", ring(count_gy, 1))
        ydn = lax.ppermute(ydn, "gy", ring(count_gy, -1))
        if last:
            send = call(
                lambda *refs: last_middle_kernel(cells_y, norm, *refs), sds((FAN, 6 * LANES)), "last_middle"
            )(recv, ta, tb, wavenumbers, pc, ps)
        else:
            send = call(lambda *refs: middle_kernel(cells_y, *refs), sds((FAN, 3 * LANES)), "middle")(
                recv, ta, tb
            )
        recv = exchange(send, wide)
        total = call(stream_kernel, sds(state.shape), "stream")(state, zup, zdn, yup, ydn)
        state, send = call(
            lambda *refs: collide_kernel(last, *refs),
            [sds(state.shape), sds((FAN if last else DEPTH, 3 * LANES))],
            "collide",
        )(recv, total, backward, forward, turn_c, turn_s)
    recv = exchange(send, wide)
    coeffs = call(coeffs_kernel, sds((2, 3, modes)), "coeffs")(recv)
    return (state.reshape(moments.shape), coeffs)


def solution(mesh):
    in_specs = (P(None, "gz", "gy", None), P(), P())
    out_specs = (P(None, "gz", "gy", None), P())
    return jax.shard_map(
        per_device, mesh=mesh, in_specs=in_specs, out_specs=out_specs, check_vma=False
    )
```

```python
import itertools
import math

import jax
import jax.numpy as jnp
import ml_dtypes
import numpy as np
from jax import lax
from jax.experimental import pallas as pl
from jax.experimental.pallas import tpu as pltpu
from jax.sharding import PartitionSpec as P

KMAX = 32
STEPS = 3
RELAX_RATE = 1.6
FORCE_GAIN = 0.5
LANES = 128
MOVES = (1, -1, 0)
F32 = jnp.float32
BF16 = jnp.bfloat16

PART_SIZES = {"xl": 2, "z": 16, "c": 2, "xh": 2, "y": 4}
DEPTH = 16
FAN = 32

PAIR_LIST = ((0, 0), (1, 1), (2, 2), (0, 1), (0, 2), (1, 2))
PAIR_INDEX = {(0, 1): 7, (0, 2): 8, (1, 2): 9}


def device_groups(axes):
    others = [a for a in PART_SIZES if a not in axes]
    groups = []
    for outer in itertools.product(*[range(PART_SIZES[a]) for a in others]):
        group = []
        for inner in itertools.product(*[range(PART_SIZES[a]) for a in axes]):
            at = dict(zip(others, outer))
            at.update(zip(axes, inner))
            gy = at["xl"] * 32 + at["z"] * 2 + at["c"]
            gz = at["xh"] * 4 + at["y"]
            group.append(gy * 8 + gz)
        groups.append(group)
    return groups


def split_np(values):
    high = values.astype(ml_dtypes.bfloat16)
    low = (values - high.astype(np.float64)).astype(ml_dtypes.bfloat16)
    return high, low


def split(value):
    high = value.astype(BF16)
    low = (value - high.astype(F32)).astype(BF16)
    return high, low


def static_tables(cells_x, cells_y, cells_z):
    wave = np.arange(KMAX)
    lane = np.arange(LANES)
    rows = cells_x // LANES
    angle = 2.0 * np.pi * (lane[:, None] * wave[None, :] % cells_x) / cells_x
    basis = np.concatenate([np.cos(angle), np.sin(angle)], axis=1)
    high, low = split_np(basis)
    forward = np.concatenate([high, high, low, low], axis=1)
    backward = np.concatenate(
        [np.concatenate([high.T, high.T], axis=0), np.concatenate([low.T, low.T], axis=0)], axis=1
    )
    row = np.arange(rows)
    turn = 2.0 * np.pi * (row[:, None] * LANES * wave[None, :] % cells_x) / cells_x
    turn_c = np.tile(np.cos(turn), (1, 4))
    turn_s = np.concatenate([-np.sin(turn), np.sin(turn)] * 2, axis=1)
    turns = np.stack([turn_c, turn_s]).astype(np.float32)
    angle = 2.0 * np.pi * (np.arange(cells_y)[:, None] * wave[None, :] % cells_y) / cells_y
    rotate = np.concatenate(
        [
            np.concatenate([np.cos(angle), -np.sin(angle)], axis=1),
            np.concatenate([np.sin(angle), np.cos(angle)], axis=1),
        ],
        axis=0,
    )
    high, low = split_np(rotate)
    rotate = np.concatenate([high, high, low, np.zeros_like(low)], axis=1)
    return np.concatenate([forward, backward, rotate], axis=0), turns


def send_row(send_ref, row):
    send_ref[...] = jnp.broadcast_to(row[None], send_ref.shape)


def lane_index(shape):
    return lax.broadcasted_iota(jnp.int32, shape, len(shape) - 1)


def call(kernel, out_shapes, name, micros=1):
    single = not isinstance(out_shapes, (list, tuple))
    shapes = [out_shapes] if single else list(out_shapes)
    spec = pl.BlockSpec(memory_space=pltpu.VMEM)
    return pl.pallas_call(
        kernel,
        out_shape=out_shapes if single else tuple(shapes),
        out_specs=spec if single else tuple(spec for _ in shapes),
        compiler_params=pltpu.CompilerParams(vmem_limit_bytes=40 * 1024 * 1024),
        cost_estimate=pl.CostEstimate(
            flops=micros * 1_000_000, bytes_accessed=micros * 3_000_000, transcendentals=0
        ),
        name=name,
    )


def forward_of(basis_ref):
    return basis_ref[0:LANES, :]


def backward_of(basis_ref):
    return basis_ref[LANES : 2 * LANES, :]


def sds(shape, dtype=F32):
    return jax.ShapeDtypeStruct(shape, dtype)


def setup_kernel(scale, sizes, waves_ref, gain_ref, basis_ref, ta_ref, tb_ref, pc_ref, ps_ref):
    cells_y, cells_z = sizes
    modes = gain_ref.shape[1]
    k_x = waves_ref[0:1, :]
    k_y = waves_ref[1:2, :]
    k_z = waves_ref[2:3, :]
    cell = lax.rem(k_z, cells_z) * KMAX + k_y
    columns = KMAX * cells_z
    hot_yz = (lax.broadcasted_iota(jnp.int32, (columns, modes), 0) == cell).astype(F32).astype(BF16)
    wave_row = lax.rem(lax.broadcasted_iota(jnp.int32, (LANES, modes), 0), KMAX)
    gains = jnp.where(wave_row == k_x, gain_ref[0:1, :] * scale, 0.0)
    gain_high, gain_low = split(gains)
    dims = (((1,), (1,)), ((), ()))
    spectrum = lax.dot_general(hot_yz, gain_high, dims, preferred_element_type=F32)
    spectrum = spectrum + lax.dot_general(hot_yz, gain_low, dims, preferred_element_type=F32)
    bands = [spectrum[k * KMAX : (k + 1) * KMAX] for k in range(cells_z)]
    half = cells_z // 2
    evens = [bands[k] + bands[cells_z - k] for k in range(1, half)]
    odds = [bands[k] - bands[cells_z - k] for k in range(1, half)]
    rotate = basis_ref[2 * LANES : 3 * LANES, 0 : 6 * KMAX]
    along_c = []
    along_s = []
    for d_z in range(cells_z):
        mirror = min(d_z, cells_z - d_z)
        if mirror == d_z:
            cos_sum = bands[0] + bands[half] if d_z % 2 == 0 else bands[0] - bands[half]
            sin_sum = jnp.zeros_like(cos_sum)
            for k in range(1, half):
                angle = 2.0 * math.pi * (k * d_z % cells_z) / cells_z
                cos_sum = cos_sum + math.cos(angle) * evens[k - 1]
                if d_z % half != 0:
                    sin_sum = sin_sum + math.sin(angle) * odds[k - 1]
            pair = (cos_sum, sin_sum)
            along_c.append(pair)
        else:
            pair = (along_c[mirror][0], -along_c[mirror][1])
        high, low = split(jnp.concatenate(pair, axis=0))
        along_s.append(
            jnp.dot(rotate, jnp.concatenate([high, low, high], axis=0), preferred_element_type=F32)
        )
    lanes = lane_index((cells_y, LANES))
    lower = lanes < LANES // 2
    sign = jnp.where(lax.rem(lanes, 2 * KMAX) < KMAX, 1.0, -1.0)
    for d_z in range(cells_z):
        here = along_s[d_z]
        before = along_s[(d_z - 1) % cells_z]
        ta_ref[:, d_z % 2, d_z // 2, :] = jnp.where(lower, here[:cells_y], before[:cells_y])
        tb_ref[:, d_z % 2, d_z // 2, :] = sign * jnp.where(lower, here[cells_y:], before[cells_y:])
    gy = lax.axis_index("gy")
    gz = lax.axis_index("gz")
    row = lax.broadcasted_iota(jnp.int32, (2 * DEPTH, modes), 0)
    y_pos = (gy // 32) * 32 + lax.rem(gy, 2) + 2 * lax.rem(row, DEPTH)
    z_pos = 2 * gz + row // DEPTH
    turns = lax.rem(y_pos * k_y, cells_y).astype(F32) / cells_y
    turns = turns + lax.rem(z_pos * k_z, cells_z).astype(F32) / cells_z
    phase = 2.0 * math.pi * turns
    pc_ref[...] = jnp.cos(phase)
    ps_ref[...] = jnp.sin(phase)


def project(velocity, basis_ref, turns_ref):
    stacked = jnp.concatenate(velocity, axis=0)
    high, low = split(stacked)
    both = jnp.concatenate([high, low], axis=0)
    product = jnp.dot(both, forward_of(basis_ref), preferred_element_type=F32)
    count = stacked.shape[0]
    base = product[:count, :LANES] + product[count:, :LANES]
    base = base + (product[:count, LANES:] + product[count:, LANES:])
    swapped = pltpu.roll(base, KMAX, 1)
    rows = turns_ref.shape[1]
    turn_c = turns_ref[0]
    turn_s = turns_ref[1]
    lower = lane_index((1, LANES)) < LANES // 2
    parts = []
    for comp in range(3):
        sums = []
        for layer in range(2):
            start = (2 * comp + layer) * rows
            term = base[start : start + rows] * turn_c + swapped[start : start + rows] * turn_s
            sums.append(jnp.sum(term, axis=0, keepdims=True))
        parts.append(jnp.where(lower, sums[0], sums[1]))
    return jnp.concatenate(parts, axis=1)


def first_kernel(state_ref, basis_ref, turns_ref, send_ref):
    inverse = 1.0 / state_ref[0]
    velocity = [state_ref[1 + comp] * inverse for comp in range(3)]
    row = project(velocity, basis_ref, turns_ref)
    send_row(send_ref, row)


def convolve(recv_ref, ta_ref, tb_ref, cells_y):
    gy = lax.axis_index("gy")
    own_xl = gy // 32
    own_z = lax.rem(gy, 32) // 2
    own_c = lax.rem(gy, 2)
    lanes = lane_index((DEPTH, LANES))
    first = lax.rem(lanes, 2 * KMAX) < KMAX
    direct = []
    swapped = []
    for comp in range(3):
        block = recv_ref[:, 0, comp * LANES : (comp + 1) * LANES]
        direct.append(block)
        swapped.append(jnp.where(first, pltpu.roll(block, LANES - KMAX, 1), pltpu.roll(block, KMAX, 1)))
    acc = {}
    for source in range(DEPTH):
        d_row = [jnp.broadcast_to(direct[comp][source : source + 1, :], (8, LANES)) for comp in range(3)]
        s_row = [jnp.broadcast_to(swapped[comp][source : source + 1, :], (8, LANES)) for comp in range(3)]
        for j, (xl, c) in enumerate(itertools.product(range(2), range(2))):
            shift = 32 * (xl - own_xl) + 2 * (own_z - source) + (c - own_c)
            shift = lax.rem(shift + 2 * cells_y, cells_y)
            for par in range(2):
                t_a = ta_ref[shift, par]
                t_b = tb_ref[shift, par]
                for comp in range(3):
                    term = t_a * d_row[comp] + t_b * s_row[comp]
                    key = (j, par, comp)
                    acc[key] = term if source == 0 else acc[key] + term
    return acc


def write_partial(acc, move, send_ref):
    gz = lax.axis_index("gz")
    lower = lane_index((8, LANES)) < LANES // 2
    for j in range(4):
        for comp in range(3):
            even = acc[(j, 0, comp)]
            odd = acc[(j, 1, comp)]
            even = even + pltpu.roll(even, LANES // 2, 1)
            odd = odd + pltpu.roll(odd, LANES // 2, 1)
            if move > 0:
                even, odd = odd, pltpu.roll(even, 7, 0)
            elif move < 0:
                even, odd = pltpu.roll(odd, 1, 0), even
            block = pltpu.roll(jnp.where(lower, even, odd), gz, 0)
            send_ref[j * 8 : (j + 1) * 8, 0, comp * LANES : (comp + 1) * LANES] = block


def middle_kernel(cells_y, move, recv_ref, ta_ref, tb_ref, send_ref):
    write_partial(convolve(recv_ref, ta_ref, tb_ref, cells_y), move, send_ref)
    send_ref[:, :, 3 * LANES :] = jnp.zeros((FAN, 1, 3 * LANES), F32)


def last_middle_kernel(cells_y, norm, recv_ref, ta_ref, tb_ref, waves_ref, pc_ref, ps_ref, send_ref):
    write_partial(convolve(recv_ref, ta_ref, tb_ref, cells_y), 0, send_ref)
    modes = waves_ref.shape[1]
    lanes = lane_index((DEPTH, LANES)) // KMAX
    blocks = []
    for comp in range(3):
        block = recv_ref[:, 0, comp * LANES : (comp + 1) * LANES]
        for part in range(4):
            blocks.append(jnp.where(lanes == part, block, 0.0))
    stacked = jnp.concatenate(blocks, axis=0)
    high, low = split(stacked)
    both = jnp.concatenate([high, low], axis=0)
    wave_row = lax.rem(lax.broadcasted_iota(jnp.int32, (LANES, modes), 0), KMAX)
    hot = (wave_row == waves_ref[0:1, :]).astype(F32).astype(BF16)
    picked = jnp.dot(both, hot, preferred_element_type=F32)
    count = stacked.shape[0]
    picked = picked[:count] + picked[count:]
    for comp in range(3):
        cos_sum = None
        sin_sum = None
        for layer in range(2):
            start = (comp * 4 + layer * 2) * DEPTH
            cos_x = picked[start : start + DEPTH]
            sin_x = picked[start + DEPTH : start + 2 * DEPTH]
            cos_yz = pc_ref[layer * DEPTH : (layer + 1) * DEPTH, :]
            sin_yz = ps_ref[layer * DEPTH : (layer + 1) * DEPTH, :]
            cos_term = cos_x * cos_yz - sin_x * sin_yz
            sin_term = sin_x * cos_yz + cos_x * sin_yz
            cos_sum = cos_term if cos_sum is None else cos_sum + cos_term
            sin_sum = sin_term if sin_sum is None else sin_sum + sin_term
        for part, total in ((0, cos_sum), (1, sin_sum)):
            total = jnp.sum(total, axis=0, keepdims=True) * norm
            for tile in range(modes // LANES):
                index = (part * 3 + comp) * (modes // LANES) + tile
                dest, slot = divmod(index, 3)
                send_ref[dest, :, (3 + slot) * LANES : (4 + slot) * LANES] = total[
                    :, tile * LANES : (tile + 1) * LANES
                ]


def weight(velocity):
    total = sum(abs(v) for v in velocity)
    return (1.0 / 3.0, 1.0 / 18.0, 1.0 / 36.0)[total]


class Populations:
    def __init__(self, fields):
        self.fields = fields
        third = fields[0] * (1.0 / 3.0)
        self.normal = [fields[4 + comp] - third for comp in range(3)]
        self.trace = (self.normal[0] + self.normal[1] + self.normal[2]) * (1.0 / 3.0)
        self.halves = {}

    def half(self, velocity):
        if velocity not in self.halves:
            quad = -self.trace
            flow = None
            used = [comp for comp in range(3) if velocity[comp] != 0]
            for comp in used:
                quad = quad + self.normal[comp]
                term = self.fields[1 + comp] if velocity[comp] > 0 else -self.fields[1 + comp]
                flow = term if flow is None else flow + term
            if len(used) == 2:
                factor = 2.0 * velocity[used[0]] * velocity[used[1]]
                quad = quad + factor * self.fields[PAIR_INDEX[tuple(used)]]
            w = weight(velocity)
            even = w * self.fields[0] + (4.5 * w) * quad
            odd = None if flow is None else (3.0 * w) * flow
            self.halves[velocity] = (even, odd)
        return self.halves[velocity]

    def get(self, velocity):
        flip = next((v < 0 for v in velocity if v != 0), False)
        key = tuple(-v for v in velocity) if flip else velocity
        even, odd = self.half(key)
        value = even if odd is None else (even - odd if flip else even + odd)
        if velocity[0] == 0:
            return value
        rows = value.shape[0]
        lanes = lane_index(value.shape)
        if velocity[0] > 0:
            moved = pltpu.roll(value, 1, 1)
            return jnp.where(lanes == 0, pltpu.roll(moved, 1, 0), moved)
        moved = pltpu.roll(value, LANES - 1, 1)
        return jnp.where(lanes == LANES - 1, pltpu.roll(moved, rows - 1, 0), moved)


def layers(state_ref):
    rows = state_ref.shape[1] // 2
    return [
        Populations([state_ref[field, layer * rows : (layer + 1) * rows, :] for field in range(10)])
        for layer in range(2)
    ]


def face_z(sign):
    return ((0, 0, sign), (1, 0, sign), (-1, 0, sign), (0, 1, sign), (0, -1, sign))


def face_y(sign):
    return ((0, sign, 0), (1, sign, 0), (-1, sign, 0))


class Received:
    def __init__(self, ref, start, sign):
        self.places = {velocity: start + index for index, velocity in enumerate(face_z(sign))}
        self.ref = ref

    def get(self, velocity):
        return self.ref[self.places[velocity]]


def sources(move, state_ref, halo_refs):
    low, high = layers(state_ref)
    if move == 0:
        below = Received(halo_refs[0], 0, 1)
        above = Received(halo_refs[1], 0, -1)
        return (low, below, high), (high, low, above)
    inner = Populations([halo_refs[0][field] for field in range(10)])
    outer = Received(halo_refs[0], 10, -move)
    if move > 0:
        return (high, low, inner), (inner, high, outer)
    return (inner, outer, low), (low, inner, high)


def halo_kernel(move, state_ref, *send_refs):
    low, high = layers(state_ref)
    if move == 0:
        for layer, sign, ref in ((high, 1, send_refs[0]), (low, -1, send_refs[1])):
            for index, velocity in enumerate(face_z(sign)):
                ref[index] = layer.get(velocity)
        return
    near, far = (low, high) if move > 0 else (high, low)
    for field in range(10):
        send_refs[0][field] = near.fields[field]
    for index, velocity in enumerate(face_z(-move)):
        send_refs[0][10 + index] = far.get(velocity)


def pack_kernel(move, state_ref, *refs):
    yup_ref, ydn_ref = refs[-2:]
    for layer, (centre, below, above) in enumerate(sources(move, state_ref, refs[:-2])):
        for sign, ref in ((1, yup_ref), (-1, ydn_ref)):
            for index, velocity in enumerate(face_y(sign)):
                ref[5 * layer + index] = centre.get(velocity)
            ref[5 * layer + 3] = below.get((0, sign, 1))
            ref[5 * layer + 4] = above.get((0, sign, -1))


def stream_kernel(move, state_ref, *refs):
    yup_ref, ydn_ref, total_ref = refs[-3:]
    rows = state_ref.shape[1] // 2
    for layer, (centre, below, above) in enumerate(sources(move, state_ref, refs[:-3])):
        terms = {}
        for shift in (0, 1, -1):
            terms[(shift, 0, 0)] = centre.get((shift, 0, 0))
            terms[(shift, 0, 1)] = below.get((shift, 0, 1))
            terms[(shift, 0, -1)] = above.get((shift, 0, -1))
        for sign, ref in ((1, yup_ref), (-1, ydn_ref)):
            for index, velocity in enumerate(face_y(sign) + ((0, sign, 1), (0, sign, -1))):
                terms[velocity] = ref[5 * layer + index]
        total = [None] * 10

        def add(index, value, factor=1):
            if factor < 0:
                total[index] = -value if total[index] is None else total[index] - value
            else:
                total[index] = value if total[index] is None else total[index] + value

        for velocity, value in terms.items():
            add(0, value)
            for comp in range(3):
                if velocity[comp] != 0:
                    add(1 + comp, value, velocity[comp])
            for index, (comp_a, comp_b) in enumerate(PAIR_LIST):
                product = velocity[comp_a] * velocity[comp_b]
                if product != 0:
                    add(4 + index, value, product)
        for index in range(10):
            total_ref[index, layer * rows : (layer + 1) * rows, :] = total[index]


def expand(row, basis_ref, turns_ref):
    turn_c = turns_ref[0]
    turn_s = turns_ref[1]
    lower = lane_index((1, LANES)) < LANES // 2
    blocks = []
    for comp in range(3):
        pair = row[:, comp * LANES : (comp + 1) * LANES]
        other = pltpu.roll(pair, LANES // 2, 1)
        for value in (jnp.where(lower, pair, other), jnp.where(lower, other, pair)):
            blocks.append(value * turn_c - pltpu.roll(value, KMAX, 1) * turn_s)
    stacked = jnp.concatenate(blocks, axis=0)
    high = stacked.astype(BF16).astype(F32)
    mixed = jnp.where(lane_index(stacked.shape) < LANES // 2, high, stacked - high).astype(BF16)
    product = jnp.dot(mixed, backward_of(basis_ref), preferred_element_type=F32)
    return product[:, :LANES] + product[:, LANES:]


def collide_kernel(
    last, recv_ref, total_ref, basis_ref, turns_ref, state_ref, send_ref
):
    row = jnp.sum(recv_ref[...], axis=0)
    force = expand(row[:, : 3 * LANES], basis_ref, turns_ref)
    cells = total_ref.shape[1]
    density = total_ref[0]
    inverse = 1.0 / density
    state_ref[0] = density
    shifted = []
    velocity = []
    for comp in range(3):
        part = force[comp * cells : (comp + 1) * cells]
        flow = total_ref[1 + comp]
        shifted.append((flow + 0.5 * part) * inverse)
        flow = flow + part
        state_ref[1 + comp] = flow
        velocity.append(flow * inverse)
    for index, (comp_a, comp_b) in enumerate(PAIR_LIST):
        equilibrium = density * shifted[comp_a] * shifted[comp_b]
        if comp_a == comp_b:
            equilibrium = equilibrium + density * (1.0 / 3.0)
        state_ref[4 + index] = equilibrium + (1.0 - RELAX_RATE) * (total_ref[4 + index] - equilibrium)
    if last:
        send_row(send_ref, row[:, 3 * LANES :])
    else:
        row = project(velocity, basis_ref, turns_ref)
        send_row(send_ref, row)


def coeffs_kernel(recv_ref, out_ref):
    tiles = out_ref.shape[2] // LANES
    for part in range(2):
        for comp in range(3):
            for tile in range(tiles):
                dest, slot = divmod((part * 3 + comp) * tiles + tile, 3)
                out_ref[comp, part : part + 1, tile * LANES : (tile + 1) * LANES] = recv_ref[
                    dest, :, slot * LANES : (slot + 1) * LANES
                ]


def ring(count, step):
    return [(index, (index + step) % count) for index in range(count)]


def per_device(moments, wavenumbers, mode_gain):
    depth, rows, cells_x = moments.shape[1:]
    modes = mode_gain.shape[0]
    count_gy = lax.axis_size("gy")
    count_gz = lax.axis_size("gz")
    cells_y = rows * count_gy
    cells_z = depth * count_gz
    x_rows = cells_x // LANES
    norm = 1.0 / math.sqrt(cells_x * cells_y * cells_z)
    force_scale = FORCE_GAIN / math.sqrt(2 * modes * count_gy * count_gz)
    basis, turns = [jnp.asarray(t) for t in static_tables(cells_x, cells_y, cells_z)]
    state = moments.reshape(10, depth * x_rows, LANES)
    deep = device_groups(["z"])
    wide = device_groups(["xl", "c", "xh", "y"])

    def exchange(value, groups):
        return lax.all_to_all(value, ("gy", "gz"), 0, 0, tiled=True, axis_index_groups=groups)

    layer = (x_rows, LANES)
    send = call(first_kernel, sds((DEPTH, 1, 3 * LANES)), "first")(state, basis, turns)
    ta, tb, pc, ps = call(
        lambda *refs: setup_kernel(norm * force_scale, (cells_y, cells_z), *refs),
        [sds((cells_y, 2, 8, LANES))] * 2 + [sds((2 * DEPTH, modes))] * 2,
        "setup",
    )(wavenumbers, mode_gain.reshape(1, modes), basis)
    for step, move in enumerate(MOVES):
        last = step == STEPS - 1
        halo_shapes = [sds((15,) + layer)] if move else [sds((5,) + layer)] * 2
        halos = call(lambda *refs: halo_kernel(move, *refs), halo_shapes, "halo")(state)
        shifts = (-move,) if move else (1, -1)
        halos = [lax.ppermute(h, "gz", ring(count_gz, shift)) for h, shift in zip(halos, shifts)]
        recv = exchange(send, deep)
        yup, ydn = call(lambda *refs: pack_kernel(move, *refs), [sds((10,) + layer)] * 2, "pack")(
            state, *halos
        )
        yup = lax.ppermute(yup, "gy", ring(count_gy, 1))
        ydn = lax.ppermute(ydn, "gy", ring(count_gy, -1))
        wide_shape = sds((FAN, 1, 6 * LANES))
        if last:
            send = call(
                lambda *refs: last_middle_kernel(cells_y, norm, *refs), wide_shape, "last_middle"
            )(recv, ta, tb, wavenumbers, pc, ps)
        else:
            send = call(lambda *refs: middle_kernel(cells_y, move, *refs), wide_shape, "middle")(
                recv, ta, tb
            )
        recv = exchange(send, wide)
        total = call(lambda *refs: stream_kernel(move, *refs), sds(state.shape), "stream")(
            state, *halos, yup, ydn
        )
        state, send = call(
            lambda *refs: collide_kernel(last, *refs),
            [sds(state.shape), sds((FAN if last else DEPTH, 1, 3 * LANES))],
            "collide",
        )(recv, total, basis, turns)
    recv = exchange(send, wide)
    coeffs = call(coeffs_kernel, sds((3, 2, modes)), "coeffs")(recv)
    return (state.reshape(moments.shape), jnp.transpose(coeffs, (1, 0, 2)))


def solution(mesh):
    in_specs = (P(None, "gz", "gy", None), P(), P())
    out_specs = (P(None, "gz", "gy", None), P())
    return jax.shard_map(
        per_device, mesh=mesh, in_specs=in_specs, out_specs=out_specs, check_vma=False
    )
```

```python
import itertools
import math

import jax
import jax.numpy as jnp
import ml_dtypes
import numpy as np
from jax import lax
from jax.experimental import pallas as pl
from jax.experimental.pallas import tpu as pltpu
from jax.sharding import PartitionSpec as P

KMAX = 32
STEPS = 3
RELAX_RATE = 1.6
FORCE_GAIN = 0.5
LANES = 128
MOVES = (1, -1, 0)
F32 = jnp.float32
BF16 = jnp.bfloat16

PART_SIZES = {"xl": 2, "z": 16, "c": 2, "xh": 2, "y": 4}
DEPTH = 16
OWNERS = 8
SLOTS = 12
FAN = 32

PAIR_LIST = ((0, 0), (1, 1), (2, 2), (0, 1), (0, 2), (1, 2))
PAIR_INDEX = {(0, 1): 7, (0, 2): 8, (1, 2): 9}


def device_groups(axes):
    others = [a for a in PART_SIZES if a not in axes]
    groups = []
    for outer in itertools.product(*[range(PART_SIZES[a]) for a in others]):
        group = []
        for inner in itertools.product(*[range(PART_SIZES[a]) for a in axes]):
            at = dict(zip(others, outer))
            at.update(zip(axes, inner))
            gy = at["xl"] * 32 + at["z"] * 2 + at["c"]
            gz = at["xh"] * 4 + at["y"]
            group.append(gy * 8 + gz)
        groups.append(group)
    return groups


def split_np(values):
    high = values.astype(ml_dtypes.bfloat16)
    low = (values - high.astype(np.float64)).astype(ml_dtypes.bfloat16)
    return high, low


def split(value):
    high = value.astype(BF16)
    low = (value - high.astype(F32)).astype(BF16)
    return high, low


def static_tables(cells_x, cells_y, cells_z):
    wave = np.arange(KMAX)
    lane = np.arange(LANES)
    rows = cells_x // LANES
    angle = 2.0 * np.pi * (lane[:, None] * wave[None, :] % cells_x) / cells_x
    basis = np.concatenate([np.cos(angle), np.sin(angle)], axis=1)
    high, low = split_np(basis)
    forward = np.concatenate([high, high, low, low], axis=1)
    backward = np.concatenate(
        [np.concatenate([high.T, high.T], axis=0), np.concatenate([low.T, low.T], axis=0)], axis=1
    )
    row = np.arange(rows)
    turn = 2.0 * np.pi * (row[:, None] * LANES * wave[None, :] % cells_x) / cells_x
    turn_c = np.tile(np.cos(turn), (1, 4))
    turn_s = np.concatenate([-np.sin(turn), np.sin(turn)] * 2, axis=1)
    turns = np.stack([turn_c, turn_s]).astype(np.float32)
    angle = 2.0 * np.pi * (np.arange(cells_y)[:, None] * wave[None, :] % cells_y) / cells_y
    rotate = np.concatenate(
        [
            np.concatenate([np.cos(angle), -np.sin(angle)], axis=1),
            np.concatenate([np.sin(angle), np.cos(angle)], axis=1),
        ],
        axis=0,
    )
    high, low = split_np(rotate)
    rotate = np.concatenate([high, high, low, np.zeros_like(low)], axis=1)
    return np.concatenate([forward, backward, rotate], axis=0), turns


def send_row(send_ref, row):
    send_ref[...] = jnp.broadcast_to(row[None], send_ref.shape)


def lane_index(shape):
    return lax.broadcasted_iota(jnp.int32, shape, len(shape) - 1)


def call(kernel, out_shapes, name, micros=1):
    single = not isinstance(out_shapes, (list, tuple))
    shapes = [out_shapes] if single else list(out_shapes)
    spec = pl.BlockSpec(memory_space=pltpu.VMEM)
    return pl.pallas_call(
        kernel,
        out_shape=out_shapes if single else tuple(shapes),
        out_specs=spec if single else tuple(spec for _ in shapes),
        compiler_params=pltpu.CompilerParams(vmem_limit_bytes=40 * 1024 * 1024),
        cost_estimate=pl.CostEstimate(
            flops=micros * 1_000_000, bytes_accessed=micros * 3_000_000, transcendentals=0
        ),
        name=name,
    )


def forward_of(basis_ref):
    return basis_ref[0:LANES, :]


def backward_of(basis_ref):
    return basis_ref[LANES : 2 * LANES, :]


def sds(shape, dtype=F32):
    return jax.ShapeDtypeStruct(shape, dtype)


def setup_kernel(scale, sizes, waves_ref, gain_ref, basis_ref, ta_ref, tb_ref, pc_ref, ps_ref):
    cells_y, cells_z = sizes
    modes = gain_ref.shape[1]
    k_x = waves_ref[0:1, :]
    k_y = waves_ref[1:2, :]
    k_z = waves_ref[2:3, :]
    cell = lax.rem(k_z, cells_z) * KMAX + k_y
    columns = KMAX * cells_z
    hot_yz = (lax.broadcasted_iota(jnp.int32, (columns, modes), 0) == cell).astype(F32).astype(BF16)
    wave_row = lax.rem(lax.broadcasted_iota(jnp.int32, (LANES, modes), 0), KMAX)
    gains = jnp.where(wave_row == k_x, gain_ref[0:1, :] * scale, 0.0)
    gain_high, gain_low = split(gains)
    dims = (((1,), (1,)), ((), ()))
    spectrum = lax.dot_general(hot_yz, gain_high, dims, preferred_element_type=F32)
    spectrum = spectrum + lax.dot_general(hot_yz, gain_low, dims, preferred_element_type=F32)
    bands = [spectrum[k * KMAX : (k + 1) * KMAX] for k in range(cells_z)]
    half = cells_z // 2
    evens = [bands[k] + bands[cells_z - k] for k in range(1, half)]
    odds = [bands[k] - bands[cells_z - k] for k in range(1, half)]
    rotate = basis_ref[2 * LANES : 3 * LANES, 0 : 6 * KMAX]
    along_c = []
    along_s = []
    for d_z in range(cells_z):
        mirror = min(d_z, cells_z - d_z)
        if mirror == d_z:
            cos_sum = bands[0] + bands[half] if d_z % 2 == 0 else bands[0] - bands[half]
            sin_sum = jnp.zeros_like(cos_sum)
            for k in range(1, half):
                angle = 2.0 * math.pi * (k * d_z % cells_z) / cells_z
                cos_sum = cos_sum + math.cos(angle) * evens[k - 1]
                if d_z % half != 0:
                    sin_sum = sin_sum + math.sin(angle) * odds[k - 1]
            pair = (cos_sum, sin_sum)
            along_c.append(pair)
        else:
            pair = (along_c[mirror][0], -along_c[mirror][1])
        high, low = split(jnp.concatenate(pair, axis=0))
        along_s.append(
            jnp.dot(rotate, jnp.concatenate([high, low, high], axis=0), preferred_element_type=F32)
        )
    lanes = lane_index((cells_y, LANES))
    lower = lanes < LANES // 2
    sign = jnp.where(lax.rem(lanes, 2 * KMAX) < KMAX, 1.0, -1.0)
    for d_z in range(cells_z):
        here = along_s[d_z]
        before = along_s[(d_z - 1) % cells_z]
        ta_ref[:, d_z % 2, d_z // 2, :] = jnp.where(lower, here[:cells_y], before[:cells_y])
        tb_ref[:, d_z % 2, d_z // 2, :] = sign * jnp.where(lower, here[cells_y:], before[cells_y:])
    gy = lax.axis_index("gy")
    gz = lax.axis_index("gz")
    row = lax.broadcasted_iota(jnp.int32, (2 * DEPTH, modes), 0)
    y_pos = (gy // 32) * 32 + lax.rem(gy, 2) + 2 * lax.rem(row, DEPTH)
    z_pos = 2 * gz + row // DEPTH
    turns = lax.rem(y_pos * k_y, cells_y).astype(F32) / cells_y
    turns = turns + lax.rem(z_pos * k_z, cells_z).astype(F32) / cells_z
    phase = 2.0 * math.pi * turns
    pc_ref[...] = jnp.cos(phase)
    ps_ref[...] = jnp.sin(phase)


def project(velocity, basis_ref, turns_ref):
    stacked = jnp.concatenate(velocity, axis=0)
    high, low = split(stacked)
    both = jnp.concatenate([high, low], axis=0)
    product = jnp.dot(both, forward_of(basis_ref), preferred_element_type=F32)
    count = stacked.shape[0]
    base = product[:count, :LANES] + product[count:, :LANES]
    base = base + (product[:count, LANES:] + product[count:, LANES:])
    swapped = pltpu.roll(base, KMAX, 1)
    rows = turns_ref.shape[1]
    turn_c = turns_ref[0]
    turn_s = turns_ref[1]
    lower = lane_index((1, LANES)) < LANES // 2
    parts = []
    for comp in range(3):
        sums = []
        for layer in range(2):
            start = (2 * comp + layer) * rows
            term = base[start : start + rows] * turn_c + swapped[start : start + rows] * turn_s
            sums.append(jnp.sum(term, axis=0, keepdims=True))
        parts.append(jnp.where(lower, sums[0], sums[1]))
    return jnp.concatenate(parts, axis=1)


def first_kernel(state_ref, basis_ref, turns_ref, send_ref):
    inverse = 1.0 / state_ref[0]
    velocity = [state_ref[1 + comp] * inverse for comp in range(3)]
    row = project(velocity, basis_ref, turns_ref)
    send_row(send_ref, row)


def convolve(recv_ref, ta_ref, tb_ref, cells_y):
    gy = lax.axis_index("gy")
    own_xl = gy // 32
    own_z = lax.rem(gy, 32) // 2
    own_c = lax.rem(gy, 2)
    lanes = lane_index((DEPTH, LANES))
    first = lax.rem(lanes, 2 * KMAX) < KMAX
    direct = []
    swapped = []
    for comp in range(3):
        block = recv_ref[:, 0, comp * LANES : (comp + 1) * LANES]
        direct.append(block)
        swapped.append(jnp.where(first, pltpu.roll(block, LANES - KMAX, 1), pltpu.roll(block, KMAX, 1)))
    acc = {}
    for source in range(DEPTH):
        d_row = [jnp.broadcast_to(direct[comp][source : source + 1, :], (8, LANES)) for comp in range(3)]
        s_row = [jnp.broadcast_to(swapped[comp][source : source + 1, :], (8, LANES)) for comp in range(3)]
        for j, (xl, c) in enumerate(itertools.product(range(2), range(2))):
            shift = 32 * (xl - own_xl) + 2 * (own_z - source) + (c - own_c)
            shift = lax.rem(shift + 2 * cells_y, cells_y)
            for par in range(2):
                t_a = ta_ref[shift, par]
                t_b = tb_ref[shift, par]
                for comp in range(3):
                    term = t_a * d_row[comp] + t_b * s_row[comp]
                    key = (j, par, comp)
                    acc[key] = term if source == 0 else acc[key] + term
    return acc


def write_partial(acc, move, send_ref):
    gz = lax.axis_index("gz")
    lower = lane_index((8, LANES)) < LANES // 2
    for j in range(4):
        for comp in range(3):
            even = acc[(j, 0, comp)]
            odd = acc[(j, 1, comp)]
            even = even + pltpu.roll(even, LANES // 2, 1)
            odd = odd + pltpu.roll(odd, LANES // 2, 1)
            if move > 0:
                even, odd = odd, pltpu.roll(even, 7, 0)
            elif move < 0:
                even, odd = pltpu.roll(odd, 1, 0), even
            block = pltpu.roll(jnp.where(lower, even, odd), gz, 0)
            send_ref[j * 8 : (j + 1) * 8, 0, comp * LANES : (comp + 1) * LANES] = block


def middle_kernel(cells_y, move, recv_ref, ta_ref, tb_ref, send_ref):
    write_partial(convolve(recv_ref, ta_ref, tb_ref, cells_y), move, send_ref)
    send_ref[:, :, 3 * LANES :] = jnp.zeros((FAN, 1, 3 * LANES), F32)


def last_middle_kernel(cells_y, norm, recv_ref, ta_ref, tb_ref, waves_ref, pc_ref, ps_ref, send_ref):
    write_partial(convolve(recv_ref, ta_ref, tb_ref, cells_y), 0, send_ref)
    modes = waves_ref.shape[1]
    lanes = lane_index((DEPTH, LANES)) // KMAX
    blocks = []
    for comp in range(3):
        block = recv_ref[:, 0, comp * LANES : (comp + 1) * LANES]
        for part in range(4):
            blocks.append(jnp.where(lanes == part, block, 0.0))
    stacked = jnp.concatenate(blocks, axis=0)
    high, low = split(stacked)
    both = jnp.concatenate([high, low], axis=0)
    wave_row = lax.rem(lax.broadcasted_iota(jnp.int32, (LANES, modes), 0), KMAX)
    hot = (wave_row == waves_ref[0:1, :]).astype(F32).astype(BF16)
    picked = jnp.dot(both, hot, preferred_element_type=F32)
    count = stacked.shape[0]
    picked = picked[:count] + picked[count:]
    for comp in range(3):
        cos_sum = None
        sin_sum = None
        for layer in range(2):
            start = (comp * 4 + layer * 2) * DEPTH
            cos_x = picked[start : start + DEPTH]
            sin_x = picked[start + DEPTH : start + 2 * DEPTH]
            cos_yz = pc_ref[layer * DEPTH : (layer + 1) * DEPTH, :]
            sin_yz = ps_ref[layer * DEPTH : (layer + 1) * DEPTH, :]
            cos_term = cos_x * cos_yz - sin_x * sin_yz
            sin_term = sin_x * cos_yz + cos_x * sin_yz
            cos_sum = cos_term if cos_sum is None else cos_sum + cos_term
            sin_sum = sin_term if sin_sum is None else sin_sum + sin_term
        for part, total in ((0, cos_sum), (1, sin_sum)):
            total = jnp.sum(total, axis=0, keepdims=True) * norm
            for tile in range(modes // LANES):
                index = (part * 3 + comp) * (modes // LANES) + tile
                owner, slot = divmod(index, SLOTS)
                c, y = divmod(owner, 4)
                for xl, xh in itertools.product(range(2), range(2)):
                    dest = ((xl * 2 + c) * 2 + xh) * 4 + y
                    send_ref[dest, :, (3 + slot) * LANES : (4 + slot) * LANES] = total[
                        :, tile * LANES : (tile + 1) * LANES
                    ]


def weight(velocity):
    total = sum(abs(v) for v in velocity)
    return (1.0 / 3.0, 1.0 / 18.0, 1.0 / 36.0)[total]


class Populations:
    def __init__(self, fields):
        self.fields = fields
        third = fields[0] * (1.0 / 3.0)
        self.normal = [fields[4 + comp] - third for comp in range(3)]
        self.trace = (self.normal[0] + self.normal[1] + self.normal[2]) * (1.0 / 3.0)
        self.halves = {}

    def half(self, velocity):
        if velocity not in self.halves:
            quad = -self.trace
            flow = None
            used = [comp for comp in range(3) if velocity[comp] != 0]
            for comp in used:
                quad = quad + self.normal[comp]
                term = self.fields[1 + comp] if velocity[comp] > 0 else -self.fields[1 + comp]
                flow = term if flow is None else flow + term
            if len(used) == 2:
                factor = 2.0 * velocity[used[0]] * velocity[used[1]]
                quad = quad + factor * self.fields[PAIR_INDEX[tuple(used)]]
            w = weight(velocity)
            even = w * self.fields[0] + (4.5 * w) * quad
            odd = None if flow is None else (3.0 * w) * flow
            self.halves[velocity] = (even, odd)
        return self.halves[velocity]

    def get(self, velocity):
        flip = next((v < 0 for v in velocity if v != 0), False)
        key = tuple(-v for v in velocity) if flip else velocity
        even, odd = self.half(key)
        value = even if odd is None else (even - odd if flip else even + odd)
        if velocity[0] == 0:
            return value
        rows = value.shape[0]
        lanes = lane_index(value.shape)
        if velocity[0] > 0:
            moved = pltpu.roll(value, 1, 1)
            return jnp.where(lanes == 0, pltpu.roll(moved, 1, 0), moved)
        moved = pltpu.roll(value, LANES - 1, 1)
        return jnp.where(lanes == LANES - 1, pltpu.roll(moved, rows - 1, 0), moved)


def layers(state_ref):
    rows = state_ref.shape[1] // 2
    return [
        Populations([state_ref[field, layer * rows : (layer + 1) * rows, :] for field in range(10)])
        for layer in range(2)
    ]


def face_z(sign):
    return ((0, 0, sign), (1, 0, sign), (-1, 0, sign), (0, 1, sign), (0, -1, sign))


def face_y(sign):
    return ((0, sign, 0), (1, sign, 0), (-1, sign, 0))


class Received:
    def __init__(self, ref, start, sign):
        self.places = {velocity: start + index for index, velocity in enumerate(face_z(sign))}
        self.ref = ref

    def get(self, velocity):
        return self.ref[self.places[velocity]]


class Chosen:
    def __init__(self, flag, first, second, sign):
        self.flag = flag
        self.first = Received(first, 0, sign)
        self.second = Received(second, 0, sign)

    def get(self, velocity):
        return jnp.where(self.flag, self.first.get(velocity), self.second.get(velocity))


def sources(move, state_ref, halo_refs):
    low, high = layers(state_ref)
    if move == 0:
        even = lax.rem(lax.axis_index("gz"), 2) == 0
        below = Chosen(even, halo_refs[1], halo_refs[0], 1)
        above = Chosen(even, halo_refs[0], halo_refs[1], -1)
        return (low, below, high), (high, low, above)
    inner = Populations([halo_refs[0][field] for field in range(10)])
    outer = Received(halo_refs[0], 10, -move)
    if move > 0:
        return (high, low, inner), (inner, high, outer)
    return (inner, outer, low), (low, inner, high)


def halo_kernel(move, state_ref, *send_refs):
    low, high = layers(state_ref)
    if move == 0:
        even = lax.rem(lax.axis_index("gz"), 2) == 0
        for index, (up, down) in enumerate(zip(face_z(1), face_z(-1))):
            up = high.get(up)
            down = low.get(down)
            send_refs[0][index] = jnp.where(even, up, down)
            send_refs[1][index] = jnp.where(even, down, up)
        return
    near, far = (low, high) if move > 0 else (high, low)
    for field in range(10):
        send_refs[0][field] = near.fields[field]
    for index, velocity in enumerate(face_z(-move)):
        send_refs[0][10 + index] = far.get(velocity)


def pack_kernel(move, state_ref, *refs):
    near_ref, far_ref = refs[-2:]
    even = lax.rem(lax.axis_index("gy"), 2) == 0
    for layer, (centre, below, above) in enumerate(sources(move, state_ref, refs[:-2])):
        faces = []
        for sign in (1, -1):
            faces.append([centre.get(velocity) for velocity in face_y(sign)])
            faces[-1].append(below.get((0, sign, 1)))
            faces[-1].append(above.get((0, sign, -1)))
        for index, (up, down) in enumerate(zip(*faces)):
            near_ref[5 * layer + index] = jnp.where(even, up, down)
            far_ref[5 * layer + index] = jnp.where(even, down, up)


def stream_kernel(move, state_ref, *refs):
    near_ref, far_ref, total_ref = refs[-3:]
    even = lax.rem(lax.axis_index("gy"), 2) == 0
    rows = state_ref.shape[1] // 2
    for layer, (centre, below, above) in enumerate(sources(move, state_ref, refs[:-3])):
        terms = {}
        for shift in (0, 1, -1):
            terms[(shift, 0, 0)] = centre.get((shift, 0, 0))
            terms[(shift, 0, 1)] = below.get((shift, 0, 1))
            terms[(shift, 0, -1)] = above.get((shift, 0, -1))
        names = [face_y(sign) + ((0, sign, 1), (0, sign, -1)) for sign in (1, -1)]
        for index, (up, down) in enumerate(zip(*names)):
            near = near_ref[5 * layer + index]
            far = far_ref[5 * layer + index]
            terms[up] = jnp.where(even, far, near)
            terms[down] = jnp.where(even, near, far)
        total = [None] * 10

        def add(index, value, factor=1):
            if factor < 0:
                total[index] = -value if total[index] is None else total[index] - value
            else:
                total[index] = value if total[index] is None else total[index] + value

        for velocity, value in terms.items():
            add(0, value)
            for comp in range(3):
                if velocity[comp] != 0:
                    add(1 + comp, value, velocity[comp])
            for index, (comp_a, comp_b) in enumerate(PAIR_LIST):
                product = velocity[comp_a] * velocity[comp_b]
                if product != 0:
                    add(4 + index, value, product)
        for index in range(10):
            total_ref[index, layer * rows : (layer + 1) * rows, :] = total[index]


def expand(row, basis_ref, turns_ref):
    turn_c = turns_ref[0]
    turn_s = turns_ref[1]
    lower = lane_index((1, LANES)) < LANES // 2
    blocks = []
    for comp in range(3):
        pair = row[:, comp * LANES : (comp + 1) * LANES]
        other = pltpu.roll(pair, LANES // 2, 1)
        for value in (jnp.where(lower, pair, other), jnp.where(lower, other, pair)):
            blocks.append(value * turn_c - pltpu.roll(value, KMAX, 1) * turn_s)
    stacked = jnp.concatenate(blocks, axis=0)
    high = stacked.astype(BF16).astype(F32)
    mixed = jnp.where(lane_index(stacked.shape) < LANES // 2, high, stacked - high).astype(BF16)
    product = jnp.dot(mixed, backward_of(basis_ref), preferred_element_type=F32)
    return product[:, :LANES] + product[:, LANES:]


def collide_kernel(
    last, recv_ref, total_ref, basis_ref, turns_ref, state_ref, send_ref
):
    row = jnp.sum(recv_ref[...], axis=0)
    force = expand(row[:, : 3 * LANES], basis_ref, turns_ref)
    cells = total_ref.shape[1]
    density = total_ref[0]
    inverse = 1.0 / density
    state_ref[0] = density
    shifted = []
    velocity = []
    for comp in range(3):
        part = force[comp * cells : (comp + 1) * cells]
        flow = total_ref[1 + comp]
        shifted.append((flow + 0.5 * part) * inverse)
        flow = flow + part
        state_ref[1 + comp] = flow
        velocity.append(flow * inverse)
    for index, (comp_a, comp_b) in enumerate(PAIR_LIST):
        equilibrium = density * shifted[comp_a] * shifted[comp_b]
        if comp_a == comp_b:
            equilibrium = equilibrium + density * (1.0 / 3.0)
        state_ref[4 + index] = equilibrium + (1.0 - RELAX_RATE) * (total_ref[4 + index] - equilibrium)
    if last:
        send_row(send_ref, row[:, 3 * LANES :])
    else:
        row = project(velocity, basis_ref, turns_ref)
        send_row(send_ref, row)


def coeffs_kernel(recv_ref, out_ref):
    tiles = out_ref.shape[2] // LANES
    for part in range(2):
        for comp in range(3):
            for tile in range(tiles):
                dest, slot = divmod((part * 3 + comp) * tiles + tile, SLOTS)
                out_ref[comp, part : part + 1, tile * LANES : (tile + 1) * LANES] = recv_ref[
                    dest, :, slot * LANES : (slot + 1) * LANES
                ]


def ring(count, step):
    return [(index, (index + step) % count) for index in range(count)]


def swap(count, start):
    pairs = [((index + start) % count, (index + start + 1) % count) for index in range(0, count, 2)]
    return pairs + [(high, low) for low, high in pairs]


def per_device(moments, wavenumbers, mode_gain):
    depth, rows, cells_x = moments.shape[1:]
    modes = mode_gain.shape[0]
    count_gy = lax.axis_size("gy")
    count_gz = lax.axis_size("gz")
    cells_y = rows * count_gy
    cells_z = depth * count_gz
    x_rows = cells_x // LANES
    norm = 1.0 / math.sqrt(cells_x * cells_y * cells_z)
    force_scale = FORCE_GAIN / math.sqrt(2 * modes * count_gy * count_gz)
    basis, turns = [jnp.asarray(t) for t in static_tables(cells_x, cells_y, cells_z)]
    state = moments.reshape(10, depth * x_rows, LANES)
    deep = device_groups(["z"])
    wide = device_groups(["xl", "c", "xh", "y"])

    def exchange(value, groups):
        return lax.all_to_all(value, ("gy", "gz"), 0, 0, tiled=True, axis_index_groups=groups)

    layer = (x_rows, LANES)
    send = call(first_kernel, sds((DEPTH, 1, 3 * LANES)), "first")(state, basis, turns)
    ta, tb, pc, ps = call(
        lambda *refs: setup_kernel(norm * force_scale, (cells_y, cells_z), *refs),
        [sds((cells_y, 2, 8, LANES))] * 2 + [sds((2 * DEPTH, modes))] * 2,
        "setup",
    )(wavenumbers, mode_gain.reshape(1, modes), basis)
    for step, move in enumerate(MOVES):
        last = step == STEPS - 1
        halo_shapes = [sds((15,) + layer)] if move else [sds((5,) + layer)] * 2
        halos = call(lambda *refs: halo_kernel(move, *refs), halo_shapes, "halo")(state)
        routes = [ring(count_gz, -move)] if move else [swap(count_gz, 0), swap(count_gz, 1)]
        halos = [lax.ppermute(h, "gz", route) for h, route in zip(halos, routes)]
        recv = exchange(send, deep)
        near, far = call(lambda *refs: pack_kernel(move, *refs), [sds((10,) + layer)] * 2, "pack")(
            state, *halos
        )
        near = lax.ppermute(near, "gy", swap(count_gy, 0))
        far = lax.ppermute(far, "gy", swap(count_gy, 1))
        wide_shape = sds((FAN, 1, ((3 + SLOTS) if last else 6) * LANES))
        if last:
            send = call(
                lambda *refs: last_middle_kernel(cells_y, norm, *refs), wide_shape, "last_middle"
            )(recv, ta, tb, wavenumbers, pc, ps)
        else:
            send = call(lambda *refs: middle_kernel(cells_y, move, *refs), wide_shape, "middle")(
                recv, ta, tb
            )
        recv = exchange(send, wide)
        total = call(lambda *refs: stream_kernel(move, *refs), sds(state.shape), "stream")(
            state, *halos, near, far
        )
        state, send = call(
            lambda *refs: collide_kernel(last, *refs),
            [sds(state.shape), sds((OWNERS, 1, SLOTS * LANES) if last else (DEPTH, 1, 3 * LANES))],
            "collide",
        )(recv, total, basis, turns)
    recv = exchange(send, device_groups(["c", "y"]))
    coeffs = call(coeffs_kernel, sds((3, 2, modes)), "coeffs")(recv)
    return (state.reshape(moments.shape), jnp.transpose(coeffs, (1, 0, 2)))


def solution(mesh):
    in_specs = (P(None, "gz", "gy", None), P(), P())
    out_specs = (P(None, "gz", "gy", None), P())
    return jax.shard_map(
        per_device, mesh=mesh, in_specs=in_specs, out_specs=out_specs, check_vma=False
    )
```

```python
import itertools
import math

import jax
import jax.numpy as jnp
import ml_dtypes
import numpy as np
from jax import lax
from jax.experimental import pallas as pl
from jax.experimental.pallas import tpu as pltpu
from jax.sharding import PartitionSpec as P

KMAX = 32
STEPS = 3
RELAX_RATE = 1.6
FORCE_GAIN = 0.5
LANES = 128
MOVES = (1, -1, 0)
F32 = jnp.float32
BF16 = jnp.bfloat16

PART_SIZES = {"xl": 2, "z": 16, "c": 2, "xh": 2, "y": 4}
DEPTH = 16
OWNERS = 8
SLOTS = 12
FAN = 32

PAIR_LIST = ((0, 0), (1, 1), (2, 2), (0, 1), (0, 2), (1, 2))
PAIR_INDEX = {(0, 1): 7, (0, 2): 8, (1, 2): 9}


def device_groups(axes):
    others = [a for a in PART_SIZES if a not in axes]
    groups = []
    for outer in itertools.product(*[range(PART_SIZES[a]) for a in others]):
        group = []
        for inner in itertools.product(*[range(PART_SIZES[a]) for a in axes]):
            at = dict(zip(others, outer))
            at.update(zip(axes, inner))
            gy = at["xl"] * 32 + at["z"] * 2 + at["c"]
            gz = at["xh"] * 4 + at["y"]
            group.append(gy * 8 + gz)
        groups.append(group)
    return groups


def split_np(values):
    high = values.astype(ml_dtypes.bfloat16)
    low = (values - high.astype(np.float64)).astype(ml_dtypes.bfloat16)
    return high, low


def split(value):
    high = value.astype(BF16)
    low = (value - high.astype(F32)).astype(BF16)
    return high, low


def static_tables(cells_x, cells_y, cells_z):
    wave = np.arange(KMAX)
    lane = np.arange(LANES)
    rows = cells_x // LANES
    angle = 2.0 * np.pi * (lane[:, None] * wave[None, :] % cells_x) / cells_x
    basis = np.concatenate([np.cos(angle), np.sin(angle)], axis=1)
    high, low = split_np(basis)
    forward = np.concatenate([high, high, low, low], axis=1)
    backward = np.concatenate(
        [np.concatenate([high.T, high.T], axis=0), np.concatenate([low.T, low.T], axis=0)], axis=1
    )
    row = np.arange(rows)
    turn = 2.0 * np.pi * (row[:, None] * LANES * wave[None, :] % cells_x) / cells_x
    turn_c = np.tile(np.cos(turn), (1, 4))
    turn_s = np.concatenate([-np.sin(turn), np.sin(turn)] * 2, axis=1)
    turns = np.stack([turn_c, turn_s]).astype(np.float32)
    angle = 2.0 * np.pi * (np.arange(cells_y)[:, None] * wave[None, :] % cells_y) / cells_y
    rotate = np.concatenate(
        [
            np.concatenate([np.cos(angle), -np.sin(angle)], axis=1),
            np.concatenate([np.sin(angle), np.cos(angle)], axis=1),
        ],
        axis=0,
    )
    high, low = split_np(rotate)
    rotate = np.concatenate([high, high, low, np.zeros_like(low)], axis=1)
    return np.concatenate([forward, backward, rotate], axis=0), turns


def send_row(send_ref, row):
    send_ref[...] = jnp.broadcast_to(row[None], send_ref.shape)


def lane_index(shape):
    return lax.broadcasted_iota(jnp.int32, shape, len(shape) - 1)


def call(kernel, out_shapes, name, micros=1, scratch=()):
    single = not isinstance(out_shapes, (list, tuple))
    shapes = [out_shapes] if single else list(out_shapes)
    spec = pl.BlockSpec(memory_space=pltpu.VMEM)
    return pl.pallas_call(
        kernel,
        out_shape=out_shapes if single else tuple(shapes),
        out_specs=spec if single else tuple(spec for _ in shapes),
        scratch_shapes=list(scratch),
        compiler_params=pltpu.CompilerParams(vmem_limit_bytes=40 * 1024 * 1024),
        cost_estimate=pl.CostEstimate(
            flops=micros * 1_000_000, bytes_accessed=micros * 3_000_000, transcendentals=0
        ),
        name=name,
    )


def forward_of(basis_ref):
    return basis_ref[0:LANES, :]


def backward_of(basis_ref):
    return basis_ref[LANES : 2 * LANES, :]


def sds(shape, dtype=F32):
    return jax.ShapeDtypeStruct(shape, dtype)


def setup_kernel(scale, sizes, waves_ref, gain_ref, basis_ref, ta_ref, tb_ref, pc_ref, ps_ref):
    cells_y, cells_z = sizes
    modes = gain_ref.shape[1]
    k_x = waves_ref[0:1, :]
    k_y = waves_ref[1:2, :]
    k_z = waves_ref[2:3, :]
    cell = lax.rem(k_z, cells_z) * KMAX + k_y
    columns = KMAX * cells_z
    hot_yz = (lax.broadcasted_iota(jnp.int32, (columns, modes), 0) == cell).astype(F32).astype(BF16)
    wave_row = lax.rem(lax.broadcasted_iota(jnp.int32, (LANES, modes), 0), KMAX)
    gains = jnp.where(wave_row == k_x, gain_ref[0:1, :] * scale, 0.0)
    gain_high, gain_low = split(gains)
    dims = (((1,), (1,)), ((), ()))
    spectrum = lax.dot_general(hot_yz, gain_high, dims, preferred_element_type=F32)
    spectrum = spectrum + lax.dot_general(hot_yz, gain_low, dims, preferred_element_type=F32)
    bands = [spectrum[k * KMAX : (k + 1) * KMAX] for k in range(cells_z)]
    half = cells_z // 2
    evens = [bands[k] + bands[cells_z - k] for k in range(1, half)]
    odds = [bands[k] - bands[cells_z - k] for k in range(1, half)]
    rotate = basis_ref[2 * LANES : 3 * LANES, 0 : 6 * KMAX]
    along_c = []
    along_s = []
    for d_z in range(cells_z):
        mirror = min(d_z, cells_z - d_z)
        if mirror == d_z:
            cos_sum = bands[0] + bands[half] if d_z % 2 == 0 else bands[0] - bands[half]
            sin_sum = jnp.zeros_like(cos_sum)
            for k in range(1, half):
                angle = 2.0 * math.pi * (k * d_z % cells_z) / cells_z
                cos_sum = cos_sum + math.cos(angle) * evens[k - 1]
                if d_z % half != 0:
                    sin_sum = sin_sum + math.sin(angle) * odds[k - 1]
            pair = (cos_sum, sin_sum)
            along_c.append(pair)
        else:
            pair = (along_c[mirror][0], -along_c[mirror][1])
        high, low = split(jnp.concatenate(pair, axis=0))
        along_s.append(
            jnp.dot(rotate, jnp.concatenate([high, low, high], axis=0), preferred_element_type=F32)
        )
    lanes = lane_index((cells_y, LANES))
    lower = lanes < LANES // 2
    sign = jnp.where(lax.rem(lanes, 2 * KMAX) < KMAX, 1.0, -1.0)
    for d_z in range(cells_z):
        here = along_s[d_z]
        before = along_s[(d_z - 1) % cells_z]
        ta_ref[:, d_z % 2, d_z // 2, :] = jnp.where(lower, here[:cells_y], before[:cells_y])
        tb_ref[:, d_z % 2, d_z // 2, :] = sign * jnp.where(lower, here[cells_y:], before[cells_y:])
    gy = lax.axis_index("gy")
    gz = lax.axis_index("gz")
    row = lax.broadcasted_iota(jnp.int32, (2 * DEPTH, modes), 0)
    y_pos = (gy // 32) * 32 + lax.rem(gy, 2) + 2 * lax.rem(row, DEPTH)
    z_pos = 2 * gz + row // DEPTH
    turns = lax.rem(y_pos * k_y, cells_y).astype(F32) / cells_y
    turns = turns + lax.rem(z_pos * k_z, cells_z).astype(F32) / cells_z
    phase = 2.0 * math.pi * turns
    pc_ref[...] = jnp.cos(phase)
    ps_ref[...] = jnp.sin(phase)


def project(velocity, basis_ref, turns_ref):
    stacked = jnp.concatenate(velocity, axis=0)
    high, low = split(stacked)
    both = jnp.concatenate([high, low], axis=0)
    product = jnp.dot(both, forward_of(basis_ref), preferred_element_type=F32)
    count = stacked.shape[0]
    base = product[:count, :LANES] + product[count:, :LANES]
    base = base + (product[:count, LANES:] + product[count:, LANES:])
    swapped = pltpu.roll(base, KMAX, 1)
    rows = turns_ref.shape[1]
    turn_c = turns_ref[0]
    turn_s = turns_ref[1]
    lower = lane_index((1, LANES)) < LANES // 2
    parts = []
    for comp in range(3):
        sums = []
        for layer in range(2):
            start = (2 * comp + layer) * rows
            term = base[start : start + rows] * turn_c + swapped[start : start + rows] * turn_s
            sums.append(jnp.sum(term, axis=0, keepdims=True))
        parts.append(jnp.where(lower, sums[0], sums[1]))
    return jnp.concatenate(parts, axis=1)


def first_kernel(state_ref, basis_ref, turns_ref, send_ref):
    inverse = 1.0 / state_ref[0]
    velocity = [state_ref[1 + comp] * inverse for comp in range(3)]
    row = project(velocity, basis_ref, turns_ref)
    send_row(send_ref, row)


def convolve(recv_ref, ta_ref, tb_ref, cells_y):
    gy = lax.axis_index("gy")
    own_xl = gy // 32
    own_z = lax.rem(gy, 32) // 2
    own_c = lax.rem(gy, 2)
    lanes = lane_index((DEPTH, LANES))
    first = lax.rem(lanes, 2 * KMAX) < KMAX
    direct = []
    swapped = []
    for comp in range(3):
        block = recv_ref[:, 0, comp * LANES : (comp + 1) * LANES]
        direct.append(block)
        swapped.append(jnp.where(first, pltpu.roll(block, LANES - KMAX, 1), pltpu.roll(block, KMAX, 1)))
    acc = {}
    for source in range(DEPTH):
        d_row = [jnp.broadcast_to(direct[comp][source : source + 1, :], (8, LANES)) for comp in range(3)]
        s_row = [jnp.broadcast_to(swapped[comp][source : source + 1, :], (8, LANES)) for comp in range(3)]
        for j, (xl, c) in enumerate(itertools.product(range(2), range(2))):
            shift = 32 * (xl - own_xl) + 2 * (own_z - source) + (c - own_c)
            shift = lax.rem(shift + 2 * cells_y, cells_y)
            for par in range(2):
                t_a = ta_ref[shift, par]
                t_b = tb_ref[shift, par]
                for comp in range(3):
                    term = t_a * d_row[comp] + t_b * s_row[comp]
                    key = (j, par, comp)
                    acc[key] = term if source == 0 else acc[key] + term
    return acc


def write_partial(acc, move, send_ref):
    gz = lax.axis_index("gz")
    lower = lane_index((8, LANES)) < LANES // 2
    for j in range(4):
        for comp in range(3):
            even = acc[(j, 0, comp)]
            odd = acc[(j, 1, comp)]
            even = even + pltpu.roll(even, LANES // 2, 1)
            odd = odd + pltpu.roll(odd, LANES // 2, 1)
            if move > 0:
                even, odd = odd, pltpu.roll(even, 7, 0)
            elif move < 0:
                even, odd = pltpu.roll(odd, 1, 0), even
            block = pltpu.roll(jnp.where(lower, even, odd), gz, 0)
            send_ref[j * 8 : (j + 1) * 8, 0, comp * LANES : (comp + 1) * LANES] = block


def middle_kernel(cells_y, move, recv_ref, ta_ref, tb_ref, send_ref):
    write_partial(convolve(recv_ref, ta_ref, tb_ref, cells_y), move, send_ref)
    send_ref[:, :, 3 * LANES :] = jnp.zeros((FAN, 1, send_ref.shape[2] - 3 * LANES), F32)


def last_middle_kernel(cells_y, norm, recv_ref, ta_ref, tb_ref, waves_ref, pc_ref, ps_ref, send_ref):
    write_partial(convolve(recv_ref, ta_ref, tb_ref, cells_y), 0, send_ref)
    modes = waves_ref.shape[1]
    lanes = lane_index((DEPTH, LANES)) // KMAX
    blocks = []
    for comp in range(3):
        block = recv_ref[:, 0, comp * LANES : (comp + 1) * LANES]
        for part in range(4):
            blocks.append(jnp.where(lanes == part, block, 0.0))
    stacked = jnp.concatenate(blocks, axis=0)
    high, low = split(stacked)
    both = jnp.concatenate([high, low], axis=0)
    wave_row = lax.rem(lax.broadcasted_iota(jnp.int32, (LANES, modes), 0), KMAX)
    hot = (wave_row == waves_ref[0:1, :]).astype(F32).astype(BF16)
    picked = jnp.dot(both, hot, preferred_element_type=F32)
    count = stacked.shape[0]
    picked = picked[:count] + picked[count:]
    for comp in range(3):
        cos_sum = None
        sin_sum = None
        for layer in range(2):
            start = (comp * 4 + layer * 2) * DEPTH
            cos_x = picked[start : start + DEPTH]
            sin_x = picked[start + DEPTH : start + 2 * DEPTH]
            cos_yz = pc_ref[layer * DEPTH : (layer + 1) * DEPTH, :]
            sin_yz = ps_ref[layer * DEPTH : (layer + 1) * DEPTH, :]
            cos_term = cos_x * cos_yz - sin_x * sin_yz
            sin_term = sin_x * cos_yz + cos_x * sin_yz
            cos_sum = cos_term if cos_sum is None else cos_sum + cos_term
            sin_sum = sin_term if sin_sum is None else sin_sum + sin_term
        for part, total in ((0, cos_sum), (1, sin_sum)):
            total = jnp.sum(total, axis=0, keepdims=True) * norm
            for tile in range(modes // LANES):
                index = (part * 3 + comp) * (modes // LANES) + tile
                owner, slot = divmod(index, SLOTS)
                c, y = divmod(owner, 4)
                for xl, xh in itertools.product(range(2), range(2)):
                    dest = ((xl * 2 + c) * 2 + xh) * 4 + y
                    send_ref[dest, :, (3 + slot) * LANES : (4 + slot) * LANES] = total[
                        :, tile * LANES : (tile + 1) * LANES
                    ]


def weight(velocity):
    total = sum(abs(v) for v in velocity)
    return (1.0 / 3.0, 1.0 / 18.0, 1.0 / 36.0)[total]


class Populations:
    def __init__(self, fields):
        self.fields = fields
        third = fields[0] * (1.0 / 3.0)
        self.normal = [fields[4 + comp] - third for comp in range(3)]
        self.trace = (self.normal[0] + self.normal[1] + self.normal[2]) * (1.0 / 3.0)
        self.halves = {}

    def half(self, velocity):
        if velocity not in self.halves:
            quad = -self.trace
            flow = None
            used = [comp for comp in range(3) if velocity[comp] != 0]
            for comp in used:
                quad = quad + self.normal[comp]
                term = self.fields[1 + comp] if velocity[comp] > 0 else -self.fields[1 + comp]
                flow = term if flow is None else flow + term
            if len(used) == 2:
                factor = 2.0 * velocity[used[0]] * velocity[used[1]]
                quad = quad + factor * self.fields[PAIR_INDEX[tuple(used)]]
            w = weight(velocity)
            even = w * self.fields[0] + (4.5 * w) * quad
            odd = None if flow is None else (3.0 * w) * flow
            self.halves[velocity] = (even, odd)
        return self.halves[velocity]

    def get(self, velocity):
        flip = next((v < 0 for v in velocity if v != 0), False)
        key = tuple(-v for v in velocity) if flip else velocity
        even, odd = self.half(key)
        value = even if odd is None else (even - odd if flip else even + odd)
        if velocity[0] == 0:
            return value
        rows = value.shape[0]
        lanes = lane_index(value.shape)
        if velocity[0] > 0:
            moved = pltpu.roll(value, 1, 1)
            return jnp.where(lanes == 0, pltpu.roll(moved, 1, 0), moved)
        moved = pltpu.roll(value, LANES - 1, 1)
        return jnp.where(lanes == LANES - 1, pltpu.roll(moved, rows - 1, 0), moved)


def layers(state_ref):
    rows = state_ref.shape[1] // 2
    return [
        Populations([state_ref[field, layer * rows : (layer + 1) * rows, :] for field in range(10)])
        for layer in range(2)
    ]


def face_z(sign):
    return ((0, 0, sign), (1, 0, sign), (-1, 0, sign), (0, 1, sign), (0, -1, sign))


def face_y(sign):
    return ((0, sign, 0), (1, sign, 0), (-1, sign, 0))


class Received:
    def __init__(self, ref, start, sign):
        self.places = {velocity: start + index for index, velocity in enumerate(face_z(sign))}
        self.ref = ref

    def get(self, velocity):
        return self.ref[self.places[velocity]]


class Chosen:
    def __init__(self, flag, first, second, sign):
        self.flag = flag
        self.first = Received(first, 0, sign)
        self.second = Received(second, 0, sign)

    def get(self, velocity):
        return jnp.where(self.flag, self.first.get(velocity), self.second.get(velocity))


def sources(move, state_ref, halo_refs):
    low, high = layers(state_ref)
    if move == 0:
        even = lax.rem(lax.axis_index("gz"), 2) == 0
        below = Chosen(even, halo_refs[1], halo_refs[0], 1)
        above = Chosen(even, halo_refs[0], halo_refs[1], -1)
        return (low, below, high), (high, low, above)
    inner = Populations([halo_refs[0][field] for field in range(10)])
    outer = Received(halo_refs[0], 10, -move)
    if move > 0:
        return (high, low, inner), (inner, high, outer)
    return (inner, outer, low), (low, inner, high)


def halo_kernel(move, state_ref, *send_refs):
    low, high = layers(state_ref)
    if move == 0:
        even = lax.rem(lax.axis_index("gz"), 2) == 0
        for index, (up, down) in enumerate(zip(face_z(1), face_z(-1))):
            up = high.get(up)
            down = low.get(down)
            send_refs[0][index] = jnp.where(even, up, down)
            send_refs[1][index] = jnp.where(even, down, up)
        return
    near, far = (low, high) if move > 0 else (high, low)
    for field in range(10):
        send_refs[0][field] = near.fields[field]
    for index, velocity in enumerate(face_z(-move)):
        send_refs[0][10 + index] = far.get(velocity)


def pack_kernel(move, state_ref, *refs):
    near_ref, far_ref = refs[-2:]
    even = lax.rem(lax.axis_index("gy"), 2) == 0
    for layer, (centre, below, above) in enumerate(sources(move, state_ref, refs[:-2])):
        faces = []
        for sign in (1, -1):
            faces.append([centre.get(velocity) for velocity in face_y(sign)])
            faces[-1].append(below.get((0, sign, 1)))
            faces[-1].append(above.get((0, sign, -1)))
        for index, (up, down) in enumerate(zip(*faces)):
            near_ref[5 * layer + index] = jnp.where(even, up, down)
            far_ref[5 * layer + index] = jnp.where(even, down, up)


def stream_kernel(move, state_ref, *refs):
    near_ref, far_ref, total_ref = refs[-3:]
    even = lax.rem(lax.axis_index("gy"), 2) == 0
    rows = state_ref.shape[1] // 2
    for layer, (centre, below, above) in enumerate(sources(move, state_ref, refs[:-3])):
        terms = {}
        for shift in (0, 1, -1):
            terms[(shift, 0, 0)] = centre.get((shift, 0, 0))
            terms[(shift, 0, 1)] = below.get((shift, 0, 1))
            terms[(shift, 0, -1)] = above.get((shift, 0, -1))
        names = [face_y(sign) + ((0, sign, 1), (0, sign, -1)) for sign in (1, -1)]
        for index, (up, down) in enumerate(zip(*names)):
            near = near_ref[5 * layer + index]
            far = far_ref[5 * layer + index]
            terms[up] = jnp.where(even, far, near)
            terms[down] = jnp.where(even, near, far)
        total = [None] * 10

        def add(index, value, factor=1):
            if factor < 0:
                total[index] = -value if total[index] is None else total[index] - value
            else:
                total[index] = value if total[index] is None else total[index] + value

        for velocity, value in terms.items():
            add(0, value)
            for comp in range(3):
                if velocity[comp] != 0:
                    add(1 + comp, value, velocity[comp])
            for index, (comp_a, comp_b) in enumerate(PAIR_LIST):
                product = velocity[comp_a] * velocity[comp_b]
                if product != 0:
                    add(4 + index, value, product)
        for index in range(10):
            total_ref[index, layer * rows : (layer + 1) * rows, :] = total[index]


def expand(row, basis_ref, turns_ref):
    turn_c = turns_ref[0]
    turn_s = turns_ref[1]
    lower = lane_index((1, LANES)) < LANES // 2
    blocks = []
    for comp in range(3):
        pair = row[:, comp * LANES : (comp + 1) * LANES]
        other = pltpu.roll(pair, LANES // 2, 1)
        for value in (jnp.where(lower, pair, other), jnp.where(lower, other, pair)):
            blocks.append(value * turn_c - pltpu.roll(value, KMAX, 1) * turn_s)
    stacked = jnp.concatenate(blocks, axis=0)
    high = stacked.astype(BF16).astype(F32)
    mixed = jnp.where(lane_index(stacked.shape) < LANES // 2, high, stacked - high).astype(BF16)
    product = jnp.dot(mixed, backward_of(basis_ref), preferred_element_type=F32)
    return product[:, :LANES] + product[:, LANES:]


def collide_kernel(last, move, recv_ref, basis_ref, turns_ref, *refs):
    state_ref, send_ref, total_ref = refs[-3:]
    stream_kernel(move, *refs[:-3], total_ref)
    row = jnp.sum(recv_ref[...] if last else recv_ref[:, :, : 3 * LANES], axis=0)
    force = expand(row[:, : 3 * LANES], basis_ref, turns_ref)
    cells = total_ref.shape[1]
    density = total_ref[0]
    inverse = 1.0 / density
    state_ref[0] = density
    shifted = []
    velocity = []
    for comp in range(3):
        part = force[comp * cells : (comp + 1) * cells]
        flow = total_ref[1 + comp]
        shifted.append((flow + 0.5 * part) * inverse)
        flow = flow + part
        state_ref[1 + comp] = flow
        velocity.append(flow * inverse)
    for index, (comp_a, comp_b) in enumerate(PAIR_LIST):
        equilibrium = density * shifted[comp_a] * shifted[comp_b]
        if comp_a == comp_b:
            equilibrium = equilibrium + density * (1.0 / 3.0)
        state_ref[4 + index] = equilibrium + (1.0 - RELAX_RATE) * (total_ref[4 + index] - equilibrium)
    if last:
        send_row(send_ref, row[:, 3 * LANES :])
    else:
        row = project(velocity, basis_ref, turns_ref)
        send_row(send_ref, row)


def coeffs_kernel(recv_ref, out_ref):
    tiles = out_ref.shape[2] // LANES
    for part in range(2):
        for comp in range(3):
            for tile in range(tiles):
                dest, slot = divmod((part * 3 + comp) * tiles + tile, SLOTS)
                out_ref[comp, part : part + 1, tile * LANES : (tile + 1) * LANES] = recv_ref[
                    dest, :, slot * LANES : (slot + 1) * LANES
                ]


def ring(count, step):
    return [(index, (index + step) % count) for index in range(count)]


def swap(count, start):
    pairs = [((index + start) % count, (index + start + 1) % count) for index in range(0, count, 2)]
    return pairs + [(high, low) for low, high in pairs]


def per_device(moments, wavenumbers, mode_gain):
    depth, rows, cells_x = moments.shape[1:]
    modes = mode_gain.shape[0]
    count_gy = lax.axis_size("gy")
    count_gz = lax.axis_size("gz")
    cells_y = rows * count_gy
    cells_z = depth * count_gz
    x_rows = cells_x // LANES
    norm = 1.0 / math.sqrt(cells_x * cells_y * cells_z)
    force_scale = FORCE_GAIN / math.sqrt(2 * modes * count_gy * count_gz)
    basis, turns = [jnp.asarray(t) for t in static_tables(cells_x, cells_y, cells_z)]
    state = moments.reshape(10, depth * x_rows, LANES)
    deep = device_groups(["z"])
    wide = device_groups(["xl", "c", "xh", "y"])

    def exchange(value, groups):
        return lax.all_to_all(value, ("gy", "gz"), 0, 0, tiled=True, axis_index_groups=groups)

    layer = (x_rows, LANES)
    send = call(first_kernel, sds((DEPTH, 1, 3 * LANES)), "first")(state, basis, turns)
    ta, tb, pc, ps = call(
        lambda *refs: setup_kernel(norm * force_scale, (cells_y, cells_z), *refs),
        [sds((cells_y, 2, 8, LANES))] * 2 + [sds((2 * DEPTH, modes))] * 2,
        "setup",
    )(wavenumbers, mode_gain.reshape(1, modes), basis)
    for step, move in enumerate(MOVES):
        last = step == STEPS - 1
        halo_shapes = [sds((15,) + layer)] if move else [sds((5,) + layer)] * 2
        halos = call(lambda *refs: halo_kernel(move, *refs), halo_shapes, "halo")(state)
        routes = [ring(count_gz, -move)] if move else [swap(count_gz, 0), swap(count_gz, 1)]
        halos = [lax.ppermute(h, "gz", route) for h, route in zip(halos, routes)]
        recv = exchange(send, deep)
        near, far = call(lambda *refs: pack_kernel(move, *refs), [sds((10,) + layer)] * 2, "pack")(
            state, *halos
        )
        near = lax.ppermute(near, "gy", swap(count_gy, 0))
        far = lax.ppermute(far, "gy", swap(count_gy, 1))
        wide_shape = sds((FAN, 1, ((3 + SLOTS) if last else 6) * LANES))
        if last:
            send = call(
                lambda *refs: last_middle_kernel(cells_y, norm, *refs), wide_shape, "last_middle"
            )(recv, ta, tb, wavenumbers, pc, ps)
        else:
            send = call(lambda *refs: middle_kernel(cells_y, move, *refs), wide_shape, "middle")(
                recv, ta, tb
            )
        recv = exchange(send, wide)
        state, send = call(
            lambda *refs: collide_kernel(last, move, *refs),
            [sds(state.shape), sds((OWNERS, 1, SLOTS * LANES) if last else (DEPTH, 1, 3 * LANES))],
            "collide",
            scratch=[pltpu.VMEM(state.shape, F32)],
        )(recv, basis, turns, state, *halos, near, far)
    recv = exchange(send, device_groups(["c", "y"]))
    coeffs = call(coeffs_kernel, sds((3, 2, modes)), "coeffs")(recv)
    return (state.reshape(moments.shape), jnp.transpose(coeffs, (1, 0, 2)))


def solution(mesh):
    in_specs = (P(None, "gz", "gy", None), P(), P())
    out_specs = (P(None, "gz", "gy", None), P())
    return jax.shard_map(
        per_device, mesh=mesh, in_specs=in_specs, out_specs=out_specs, check_vma=False
    )
```

```python
import itertools
import math

import jax
import jax.numpy as jnp
import ml_dtypes
import numpy as np
from jax import lax
from jax.experimental import pallas as pl
from jax.experimental.pallas import tpu as pltpu
from jax.sharding import PartitionSpec as P

KMAX = 32
STEPS = 3
RELAX_RATE = 1.6
FORCE_GAIN = 0.5
LANES = 128
MOVES = (1, -1, 0)
F32 = jnp.float32
BF16 = jnp.bfloat16

PART_SIZES = {"xl": 2, "z": 16, "c": 2, "xh": 2, "y": 4}
DEPTH = 16
OWNERS = 8
SLOTS = 12
FAN = 32

PAIR_LIST = ((0, 0), (1, 1), (2, 2), (0, 1), (0, 2), (1, 2))
PAIR_INDEX = {(0, 1): 7, (0, 2): 8, (1, 2): 9}


def device_groups(axes):
    others = [a for a in PART_SIZES if a not in axes]
    groups = []
    for outer in itertools.product(*[range(PART_SIZES[a]) for a in others]):
        group = []
        for inner in itertools.product(*[range(PART_SIZES[a]) for a in axes]):
            at = dict(zip(others, outer))
            at.update(zip(axes, inner))
            gy = at["xl"] * 32 + at["z"] * 2 + at["c"]
            gz = at["xh"] * 4 + at["y"]
            group.append(gy * 8 + gz)
        groups.append(group)
    return groups


def split_np(values):
    high = values.astype(ml_dtypes.bfloat16)
    low = (values - high.astype(np.float64)).astype(ml_dtypes.bfloat16)
    return high, low


def split(value):
    high = value.astype(BF16)
    low = (value - high.astype(F32)).astype(BF16)
    return high, low


def static_tables(cells_x, cells_y, cells_z):
    wave = np.arange(KMAX)
    lane = np.arange(LANES)
    rows = cells_x // LANES
    angle = 2.0 * np.pi * (lane[:, None] * wave[None, :] % cells_x) / cells_x
    basis = np.concatenate([np.cos(angle), np.sin(angle)], axis=1)
    high, low = split_np(basis)
    forward = np.concatenate([high, high, low, low], axis=1)
    backward = np.concatenate(
        [np.concatenate([high.T, high.T], axis=0), np.concatenate([low.T, low.T], axis=0)], axis=1
    )
    row = np.arange(rows)
    turn = 2.0 * np.pi * (row[:, None] * LANES * wave[None, :] % cells_x) / cells_x
    turn_c = np.tile(np.cos(turn), (1, 4))
    turn_s = np.concatenate([-np.sin(turn), np.sin(turn)] * 2, axis=1)
    turns = np.stack([turn_c, turn_s]).astype(np.float32)
    angle = 2.0 * np.pi * (np.arange(cells_y)[:, None] * wave[None, :] % cells_y) / cells_y
    rotate = np.concatenate(
        [
            np.concatenate([np.cos(angle), -np.sin(angle)], axis=1),
            np.concatenate([np.sin(angle), np.cos(angle)], axis=1),
        ],
        axis=0,
    )
    high, low = split_np(rotate)
    rotate = np.concatenate([high, high, low, np.zeros_like(low)], axis=1)
    return np.concatenate([forward, backward, rotate], axis=0), turns


def send_row(send_ref, row):
    send_ref[...] = jnp.broadcast_to(row[None], send_ref.shape)


def lane_index(shape):
    return lax.broadcasted_iota(jnp.int32, shape, len(shape) - 1)


def call(kernel, out_shapes, name, micros=1, scratch=()):
    single = not isinstance(out_shapes, (list, tuple))
    shapes = [out_shapes] if single else list(out_shapes)
    spec = pl.BlockSpec(memory_space=pltpu.VMEM)
    return pl.pallas_call(
        kernel,
        out_shape=out_shapes if single else tuple(shapes),
        out_specs=spec if single else tuple(spec for _ in shapes),
        scratch_shapes=list(scratch),
        compiler_params=pltpu.CompilerParams(vmem_limit_bytes=40 * 1024 * 1024),
        cost_estimate=pl.CostEstimate(
            flops=micros * 1_000_000, bytes_accessed=micros * 3_000_000, transcendentals=0
        ),
        name=name,
    )


def forward_of(basis_ref):
    return basis_ref[0:LANES, :]


def backward_of(basis_ref):
    return basis_ref[LANES : 2 * LANES, :]


def sds(shape, dtype=F32):
    return jax.ShapeDtypeStruct(shape, dtype)


def setup_kernel(scale, sizes, waves_ref, gain_ref, basis_ref, ta_ref, tb_ref, pc_ref, ps_ref):
    cells_y, cells_z = sizes
    modes = gain_ref.shape[1]
    k_x = waves_ref[0:1, :]
    k_y = waves_ref[1:2, :]
    k_z = waves_ref[2:3, :]
    cell = lax.rem(k_z, cells_z) * KMAX + k_y
    columns = KMAX * cells_z
    hot_yz = (lax.broadcasted_iota(jnp.int32, (columns, modes), 0) == cell).astype(F32).astype(BF16)
    wave_row = lax.rem(lax.broadcasted_iota(jnp.int32, (LANES, modes), 0), KMAX)
    gains = jnp.where(wave_row == k_x, gain_ref[0:1, :] * scale, 0.0)
    gain_high, gain_low = split(gains)
    dims = (((1,), (1,)), ((), ()))
    spectrum = lax.dot_general(hot_yz, gain_high, dims, preferred_element_type=F32)
    spectrum = spectrum + lax.dot_general(hot_yz, gain_low, dims, preferred_element_type=F32)
    bands = [spectrum[k * KMAX : (k + 1) * KMAX] for k in range(cells_z)]
    half = cells_z // 2
    evens = [bands[k] + bands[cells_z - k] for k in range(1, half)]
    odds = [bands[k] - bands[cells_z - k] for k in range(1, half)]
    rotate = basis_ref[2 * LANES : 3 * LANES, 0 : 6 * KMAX]
    along_c = []
    along_s = []
    for d_z in range(cells_z):
        mirror = min(d_z, cells_z - d_z)
        if mirror == d_z:
            cos_sum = bands[0] + bands[half] if d_z % 2 == 0 else bands[0] - bands[half]
            sin_sum = jnp.zeros_like(cos_sum)
            for k in range(1, half):
                angle = 2.0 * math.pi * (k * d_z % cells_z) / cells_z
                cos_sum = cos_sum + math.cos(angle) * evens[k - 1]
                if d_z % half != 0:
                    sin_sum = sin_sum + math.sin(angle) * odds[k - 1]
            pair = (cos_sum, sin_sum)
            along_c.append(pair)
        else:
            pair = (along_c[mirror][0], -along_c[mirror][1])
        high, low = split(jnp.concatenate(pair, axis=0))
        along_s.append(
            jnp.dot(rotate, jnp.concatenate([high, low, high], axis=0), preferred_element_type=F32)
        )
    lanes = lane_index((cells_y, LANES))
    lower = lanes < LANES // 2
    sign = jnp.where(lax.rem(lanes, 2 * KMAX) < KMAX, 1.0, -1.0)
    for d_z in range(cells_z):
        here = along_s[d_z]
        before = along_s[(d_z - 1) % cells_z]
        ta_ref[:, d_z % 2, d_z // 2, :] = jnp.where(lower, here[:cells_y], before[:cells_y])
        tb_ref[:, d_z % 2, d_z // 2, :] = sign * jnp.where(lower, here[cells_y:], before[cells_y:])
    gy = lax.axis_index("gy")
    gz = lax.axis_index("gz")
    row = lax.broadcasted_iota(jnp.int32, (2 * DEPTH, modes), 0)
    y_pos = (gy // 32) * 32 + lax.rem(gy, 2) + 2 * lax.rem(row, DEPTH)
    z_pos = 2 * gz + row // DEPTH
    turns = lax.rem(y_pos * k_y, cells_y).astype(F32) / cells_y
    turns = turns + lax.rem(z_pos * k_z, cells_z).astype(F32) / cells_z
    phase = 2.0 * math.pi * turns
    pc_ref[...] = jnp.cos(phase)
    ps_ref[...] = jnp.sin(phase)


def project(velocity, basis_ref, turns_ref):
    stacked = jnp.concatenate(velocity, axis=0)
    high, low = split(stacked)
    both = jnp.concatenate([high, low], axis=0)
    product = jnp.dot(both, forward_of(basis_ref), preferred_element_type=F32)
    count = stacked.shape[0]
    base = product[:count, :LANES] + product[count:, :LANES]
    base = base + (product[:count, LANES:] + product[count:, LANES:])
    swapped = pltpu.roll(base, KMAX, 1)
    rows = turns_ref.shape[1]
    turn_c = turns_ref[0]
    turn_s = turns_ref[1]
    lower = lane_index((1, LANES)) < LANES // 2
    parts = []
    for comp in range(3):
        sums = []
        for layer in range(2):
            start = (2 * comp + layer) * rows
            term = base[start : start + rows] * turn_c + swapped[start : start + rows] * turn_s
            sums.append(jnp.sum(term, axis=0, keepdims=True))
        parts.append(jnp.where(lower, sums[0], sums[1]))
    return jnp.concatenate(parts, axis=1)


def first_kernel(state_ref, basis_ref, turns_ref, send_ref):
    inverse = 1.0 / state_ref[0]
    velocity = [state_ref[1 + comp] * inverse for comp in range(3)]
    row = project(velocity, basis_ref, turns_ref)
    send_row(send_ref, row)


def convolve(recv_ref, ta_ref, tb_ref, cells_y):
    gy = lax.axis_index("gy")
    own_xl = gy // 32
    own_z = lax.rem(gy, 32) // 2
    own_c = lax.rem(gy, 2)
    lanes = lane_index((DEPTH, LANES))
    first = lax.rem(lanes, 2 * KMAX) < KMAX
    direct = []
    swapped = []
    for comp in range(3):
        block = recv_ref[:, 0, comp * LANES : (comp + 1) * LANES]
        direct.append(block)
        swapped.append(jnp.where(first, pltpu.roll(block, LANES - KMAX, 1), pltpu.roll(block, KMAX, 1)))
    acc = {}
    for source in range(DEPTH):
        d_row = [jnp.broadcast_to(direct[comp][source : source + 1, :], (8, LANES)) for comp in range(3)]
        s_row = [jnp.broadcast_to(swapped[comp][source : source + 1, :], (8, LANES)) for comp in range(3)]
        for j, (xl, c) in enumerate(itertools.product(range(2), range(2))):
            shift = 32 * (xl - own_xl) + 2 * (own_z - source) + (c - own_c)
            shift = lax.rem(shift + 2 * cells_y, cells_y)
            for par in range(2):
                t_a = ta_ref[shift, par]
                t_b = tb_ref[shift, par]
                for comp in range(3):
                    term = t_a * d_row[comp] + t_b * s_row[comp]
                    key = (j, par, comp)
                    acc[key] = term if source == 0 else acc[key] + term
    return acc


def write_partial(acc, move, send_ref):
    gz = lax.axis_index("gz")
    lower = lane_index((8, LANES)) < LANES // 2
    for j in range(4):
        for comp in range(3):
            even = acc[(j, 0, comp)]
            odd = acc[(j, 1, comp)]
            even = even + pltpu.roll(even, LANES // 2, 1)
            odd = odd + pltpu.roll(odd, LANES // 2, 1)
            if move > 0:
                even, odd = odd, pltpu.roll(even, 7, 0)
            elif move < 0:
                even, odd = pltpu.roll(odd, 1, 0), even
            block = pltpu.roll(jnp.where(lower, even, odd), gz, 0)
            send_ref[j * 8 : (j + 1) * 8, 0, comp * LANES : (comp + 1) * LANES] = block


def middle_kernel(cells_y, move, recv_ref, ta_ref, tb_ref, send_ref):
    write_partial(convolve(recv_ref, ta_ref, tb_ref, cells_y), move, send_ref)
    send_ref[:, :, 3 * LANES :] = jnp.zeros((FAN, 1, send_ref.shape[2] - 3 * LANES), F32)


def last_middle_kernel(cells_y, norm, recv_ref, ta_ref, tb_ref, waves_ref, pc_ref, ps_ref, *refs):
    send_ref = refs[-1]
    write_partial(convolve(recv_ref, ta_ref, tb_ref, cells_y), 0, send_ref)
    modes = waves_ref.shape[1]
    lanes = lane_index((DEPTH, LANES)) // KMAX
    blocks = []
    for comp in range(3):
        block = recv_ref[:, 0, comp * LANES : (comp + 1) * LANES]
        for part in range(4):
            blocks.append(jnp.where(lanes == part, block, 0.0))
    stacked = jnp.concatenate(blocks, axis=0)
    high, low = split(stacked)
    both = jnp.concatenate([high, low], axis=0)
    wave_row = lax.rem(lax.broadcasted_iota(jnp.int32, (LANES, modes), 0), KMAX)
    hot = (wave_row == waves_ref[0:1, :]).astype(F32).astype(BF16)
    picked = jnp.dot(both, hot, preferred_element_type=F32)
    count = stacked.shape[0]
    picked = picked[:count] + picked[count:]
    for comp in range(3):
        cos_sum = None
        sin_sum = None
        for layer in range(2):
            start = (comp * 4 + layer * 2) * DEPTH
            cos_x = picked[start : start + DEPTH]
            sin_x = picked[start + DEPTH : start + 2 * DEPTH]
            cos_yz = pc_ref[layer * DEPTH : (layer + 1) * DEPTH, :]
            sin_yz = ps_ref[layer * DEPTH : (layer + 1) * DEPTH, :]
            cos_term = cos_x * cos_yz - sin_x * sin_yz
            sin_term = sin_x * cos_yz + cos_x * sin_yz
            cos_sum = cos_term if cos_sum is None else cos_sum + cos_term
            sin_sum = sin_term if sin_sum is None else sin_sum + sin_term
        for part, total in ((0, cos_sum), (1, sin_sum)):
            total = jnp.sum(total, axis=0, keepdims=True) * norm
            for tile in range(modes // LANES):
                index = (part * 3 + comp) * (modes // LANES) + tile
                owner, slot = divmod(index, SLOTS)
                c, y = divmod(owner, 4)
                for xl, xh in itertools.product(range(2), range(2)):
                    dest = ((xl * 2 + c) * 2 + xh) * 4 + y
                    send_ref[dest, :, (3 + slot) * LANES : (4 + slot) * LANES] = total[
                        :, tile * LANES : (tile + 1) * LANES
                    ]


def weight(velocity):
    total = sum(abs(v) for v in velocity)
    return (1.0 / 3.0, 1.0 / 18.0, 1.0 / 36.0)[total]


class Populations:
    def __init__(self, fields):
        self.fields = fields
        third = fields[0] * (1.0 / 3.0)
        self.normal = [fields[4 + comp] - third for comp in range(3)]
        self.trace = (self.normal[0] + self.normal[1] + self.normal[2]) * (1.0 / 3.0)
        self.halves = {}

    def half(self, velocity):
        if velocity not in self.halves:
            quad = -self.trace
            flow = None
            used = [comp for comp in range(3) if velocity[comp] != 0]
            for comp in used:
                quad = quad + self.normal[comp]
                term = self.fields[1 + comp] if velocity[comp] > 0 else -self.fields[1 + comp]
                flow = term if flow is None else flow + term
            if len(used) == 2:
                factor = 2.0 * velocity[used[0]] * velocity[used[1]]
                quad = quad + factor * self.fields[PAIR_INDEX[tuple(used)]]
            w = weight(velocity)
            even = w * self.fields[0] + (4.5 * w) * quad
            odd = None if flow is None else (3.0 * w) * flow
            self.halves[velocity] = (even, odd)
        return self.halves[velocity]

    def get(self, velocity):
        flip = next((v < 0 for v in velocity if v != 0), False)
        key = tuple(-v for v in velocity) if flip else velocity
        even, odd = self.half(key)
        value = even if odd is None else (even - odd if flip else even + odd)
        if velocity[0] == 0:
            return value
        rows = value.shape[0]
        lanes = lane_index(value.shape)
        if velocity[0] > 0:
            moved = pltpu.roll(value, 1, 1)
            return jnp.where(lanes == 0, pltpu.roll(moved, 1, 0), moved)
        moved = pltpu.roll(value, LANES - 1, 1)
        return jnp.where(lanes == LANES - 1, pltpu.roll(moved, rows - 1, 0), moved)


def layers(state_ref):
    rows = state_ref.shape[1] // 2
    return [
        Populations([state_ref[field, layer * rows : (layer + 1) * rows, :] for field in range(10)])
        for layer in range(2)
    ]


def face_z(sign):
    return ((0, 0, sign), (1, 0, sign), (-1, 0, sign), (0, 1, sign), (0, -1, sign))


def face_y(sign):
    return ((0, sign, 0), (1, sign, 0), (-1, sign, 0))


class Received:
    def __init__(self, ref, start, sign):
        self.places = {velocity: start + index for index, velocity in enumerate(face_z(sign))}
        self.ref = ref

    def get(self, velocity):
        return self.ref[self.places[velocity]]


class Chosen:
    def __init__(self, flag, first, second, sign):
        self.flag = flag
        self.first = Received(first, 0, sign)
        self.second = Received(second, 0, sign)

    def get(self, velocity):
        return jnp.where(self.flag, self.first.get(velocity), self.second.get(velocity))


def sources(move, state_ref, halo_refs):
    low, high = layers(state_ref)
    if move == 0:
        even = lax.rem(lax.axis_index("gz"), 2) == 0
        below = Chosen(even, halo_refs[1], halo_refs[0], 1)
        above = Chosen(even, halo_refs[0], halo_refs[1], -1)
        return (low, below, high), (high, low, above)
    inner = Populations([halo_refs[0][field] for field in range(10)])
    outer = Received(halo_refs[0], 10, -move)
    if move > 0:
        return (high, low, inner), (inner, high, outer)
    return (inner, outer, low), (low, inner, high)


def halo_kernel(move, state_ref, *send_refs):
    low, high = layers(state_ref)
    if move == 0:
        even = lax.rem(lax.axis_index("gz"), 2) == 0
        for index, (up, down) in enumerate(zip(face_z(1), face_z(-1))):
            up = high.get(up)
            down = low.get(down)
            send_refs[0][index] = jnp.where(even, up, down)
            send_refs[1][index] = jnp.where(even, down, up)
        return
    near, far = (low, high) if move > 0 else (high, low)
    for field in range(10):
        send_refs[0][field] = near.fields[field]
    for index, velocity in enumerate(face_z(-move)):
        send_refs[0][10 + index] = far.get(velocity)


def pack_kernel(move, state_ref, *refs):
    near_ref, far_ref = refs[-2:]
    even = lax.rem(lax.axis_index("gy"), 2) == 0
    for layer, (centre, below, above) in enumerate(sources(move, state_ref, refs[:-2])):
        faces = []
        for sign in (1, -1):
            faces.append([centre.get(velocity) for velocity in face_y(sign)])
            faces[-1].append(below.get((0, sign, 1)))
            faces[-1].append(above.get((0, sign, -1)))
        for index, (up, down) in enumerate(zip(*faces)):
            near_ref[5 * layer + index] = jnp.where(even, up, down)
            far_ref[5 * layer + index] = jnp.where(even, down, up)


def stream_kernel(move, state_ref, *refs):
    near_ref, far_ref, total_ref = refs[-3:]
    even = lax.rem(lax.axis_index("gy"), 2) == 0
    rows = state_ref.shape[1] // 2
    for layer, (centre, below, above) in enumerate(sources(move, state_ref, refs[:-3])):
        terms = {}
        for shift in (0, 1, -1):
            terms[(shift, 0, 0)] = centre.get((shift, 0, 0))
            terms[(shift, 0, 1)] = below.get((shift, 0, 1))
            terms[(shift, 0, -1)] = above.get((shift, 0, -1))
        names = [face_y(sign) + ((0, sign, 1), (0, sign, -1)) for sign in (1, -1)]
        for index, (up, down) in enumerate(zip(*names)):
            near = near_ref[5 * layer + index]
            far = far_ref[5 * layer + index]
            terms[up] = jnp.where(even, far, near)
            terms[down] = jnp.where(even, near, far)
        total = [None] * 10

        def add(index, value, factor=1):
            if factor < 0:
                total[index] = -value if total[index] is None else total[index] - value
            else:
                total[index] = value if total[index] is None else total[index] + value

        for velocity, value in terms.items():
            add(0, value)
            for comp in range(3):
                if velocity[comp] != 0:
                    add(1 + comp, value, velocity[comp])
            for index, (comp_a, comp_b) in enumerate(PAIR_LIST):
                product = velocity[comp_a] * velocity[comp_b]
                if product != 0:
                    add(4 + index, value, product)
        for index in range(10):
            total_ref[index, layer * rows : (layer + 1) * rows, :] = total[index]


def expand(row, basis_ref, turns_ref):
    turn_c = turns_ref[0]
    turn_s = turns_ref[1]
    lower = lane_index((1, LANES)) < LANES // 2
    blocks = []
    for comp in range(3):
        pair = row[:, comp * LANES : (comp + 1) * LANES]
        other = pltpu.roll(pair, LANES // 2, 1)
        for value in (jnp.where(lower, pair, other), jnp.where(lower, other, pair)):
            blocks.append(value * turn_c - pltpu.roll(value, KMAX, 1) * turn_s)
    stacked = jnp.concatenate(blocks, axis=0)
    high = stacked.astype(BF16).astype(F32)
    mixed = jnp.where(lane_index(stacked.shape) < LANES // 2, high, stacked - high).astype(BF16)
    product = jnp.dot(mixed, backward_of(basis_ref), preferred_element_type=F32)
    return product[:, :LANES] + product[:, LANES:]


def collide_kernel(last, move, recv_ref, basis_ref, turns_ref, *refs):
    total_ref = refs[-1]
    state_ref = refs[-2] if last else refs[-3]
    stream_kernel(move, *refs[: -2 if last else -3], total_ref)
    row = jnp.sum(recv_ref[:, :, : 3 * LANES], axis=0)
    force = expand(row[:, : 3 * LANES], basis_ref, turns_ref)
    cells = total_ref.shape[1]
    density = total_ref[0]
    inverse = 1.0 / density
    state_ref[0] = density
    shifted = []
    velocity = []
    for comp in range(3):
        part = force[comp * cells : (comp + 1) * cells]
        flow = total_ref[1 + comp]
        shifted.append((flow + 0.5 * part) * inverse)
        flow = flow + part
        state_ref[1 + comp] = flow
        velocity.append(flow * inverse)
    for index, (comp_a, comp_b) in enumerate(PAIR_LIST):
        equilibrium = density * shifted[comp_a] * shifted[comp_b]
        if comp_a == comp_b:
            equilibrium = equilibrium + density * (1.0 / 3.0)
        state_ref[4 + index] = equilibrium + (1.0 - RELAX_RATE) * (total_ref[4 + index] - equilibrium)
    if not last:
        row = project(velocity, basis_ref, turns_ref)
        send_row(refs[-2], row)


def parts_kernel(recv_ref, send_ref):
    send_row(send_ref, jnp.sum(recv_ref[:, :, 3 * LANES :], axis=0))


def coeffs_kernel(recv_ref, out_ref):
    tiles = out_ref.shape[2] // LANES
    for part in range(2):
        for comp in range(3):
            for tile in range(tiles):
                dest, slot = divmod((part * 3 + comp) * tiles + tile, SLOTS)
                out_ref[comp, part : part + 1, tile * LANES : (tile + 1) * LANES] = recv_ref[
                    dest, :, slot * LANES : (slot + 1) * LANES
                ]


def ring(count, step):
    return [(index, (index + step) % count) for index in range(count)]


def swap(count, start):
    pairs = [((index + start) % count, (index + start + 1) % count) for index in range(0, count, 2)]
    return pairs + [(high, low) for low, high in pairs]


def per_device(moments, wavenumbers, mode_gain):
    depth, rows, cells_x = moments.shape[1:]
    modes = mode_gain.shape[0]
    count_gy = lax.axis_size("gy")
    count_gz = lax.axis_size("gz")
    cells_y = rows * count_gy
    cells_z = depth * count_gz
    x_rows = cells_x // LANES
    norm = 1.0 / math.sqrt(cells_x * cells_y * cells_z)
    force_scale = FORCE_GAIN / math.sqrt(2 * modes * count_gy * count_gz)
    basis, turns = [jnp.asarray(t) for t in static_tables(cells_x, cells_y, cells_z)]
    state = moments.reshape(10, depth * x_rows, LANES)
    deep = device_groups(["z"])
    wide = device_groups(["xl", "c", "xh", "y"])

    def exchange(value, groups):
        return lax.all_to_all(value, ("gy", "gz"), 0, 0, tiled=True, axis_index_groups=groups)

    layer = (x_rows, LANES)
    send = call(first_kernel, sds((DEPTH, 1, 3 * LANES)), "first")(state, basis, turns)
    ta, tb, pc, ps = call(
        lambda *refs: setup_kernel(norm * force_scale, (cells_y, cells_z), *refs),
        [sds((cells_y, 2, 8, LANES))] * 2 + [sds((2 * DEPTH, modes))] * 2,
        "setup",
    )(wavenumbers, mode_gain.reshape(1, modes), basis)
    for step, move in enumerate(MOVES):
        last = step == STEPS - 1
        halo_shapes = [sds((15,) + layer)] if move else [sds((5,) + layer)] * 2
        halos = call(lambda *refs: halo_kernel(move, *refs), halo_shapes, "halo")(state)
        routes = [ring(count_gz, -move)] if move else [swap(count_gz, 0), swap(count_gz, 1)]
        halos = [lax.ppermute(h, "gz", route) for h, route in zip(halos, routes)]
        recv = exchange(send, deep)
        near, far = call(lambda *refs: pack_kernel(move, *refs), [sds((10,) + layer)] * 2, "pack")(
            state, *halos
        )
        near = lax.ppermute(near, "gy", swap(count_gy, 0))
        far = lax.ppermute(far, "gy", swap(count_gy, 1))
        wide_shape = sds((FAN, 1, ((3 + SLOTS) if last else 6) * LANES))
        if last:
            send = call(
                lambda *refs: last_middle_kernel(cells_y, norm, *refs), wide_shape, "last_middle"
            )(recv, ta, tb, wavenumbers, pc, ps, *halos)
        else:
            send = call(lambda *refs: middle_kernel(cells_y, move, *refs), wide_shape, "middle")(
                recv, ta, tb
            )
        recv = exchange(send, wide)
        found = call(
            lambda *refs: collide_kernel(last, move, *refs),
            [sds(state.shape)] + ([] if last else [sds((DEPTH, 1, 3 * LANES))]),
            "collide",
            scratch=[pltpu.VMEM(state.shape, F32)],
        )(recv, basis, turns, state, *halos, near, far)
        state = found[0]
        if last:
            send = call(parts_kernel, sds((OWNERS, 1, SLOTS * LANES)), "parts")(recv)
        else:
            send = found[1]
    recv = exchange(send, device_groups(["c", "y"]))
    coeffs = call(coeffs_kernel, sds((3, 2, modes)), "coeffs")(recv)
    return (state.reshape(moments.shape), jnp.transpose(coeffs, (1, 0, 2)))


def solution(mesh):
    in_specs = (P(None, "gz", "gy", None), P(), P())
    out_specs = (P(None, "gz", "gy", None), P())
    return jax.shard_map(
        per_device, mesh=mesh, in_specs=in_specs, out_specs=out_specs, check_vma=False
    )
```
